256 devices in a mesh: replica: 16 (over x, z_hi), fsdp: 16 (over z_lo, y, core).
Axes of the slice: x: 4, y: 4, z: 8 (z_hi: 4, z_lo: 2; z = z_hi * 2 + z_lo), core: 2. Of those that a mesh axis runs over, the one named last changes fastest.
Arguments:
- base: bfloat16 [1024, 28672], P('fsdp')
- local: bfloat16 [16, 1024, 28672], P('replica', 'fsdp')
- momentum: float32 [1024, 28672], P('fsdp', 'replica'), may hold values from -0.6 to 0.6
Outputs:
- new_params: bfloat16 [1024, 28672], P('fsdp')
- new_momentum: float32 [1024, 28672], P('fsdp', 'replica')
- grad_rms: float32 [], replicated
The draws below stay inside these ranges and needn't reach their ends.
All inputs are finite; a program needn't handle non-finite values.
Results may differ from the reference program's by a relative error of at most 0.008.
Values may be sent and summed in bfloat16 or wider, within the bound.
A program may use at most 128 MiB of HBM per device.

```python
import math
import jax
import jax.numpy as jnp
from jax import lax

FF = 28672
ROWS = 1024
REPLICAS = 16


def shared_base(key):
    return jax.random.normal(key, (ROWS, FF), jnp.float32) * 0.5


def draw_base(key, part):
    values = shared_base(key)
    return values.astype(jnp.bfloat16)


def draw_local(key, part):
    start = shared_base(key).astype(jnp.bfloat16).astype(jnp.float32)
    key = jax.random.fold_in(key, 7)
    key_rows, key_cols, key_common, key_own = jax.random.split(key, 4)
    row_rise = 1.0 + 2.0 * jnp.arange(ROWS, dtype=jnp.float32)[:, None] / max(ROWS - 1, 1)
    col_rise = 1.0 + 2.0 * jnp.arange(FF, dtype=jnp.float32)[None, :] / (FF - 1)
    row_scale = row_rise * jnp.exp(jax.random.uniform(key_rows, (ROWS, 1), jnp.float32, 0.0, math.log(10.0)))
    col_scale = col_rise * jnp.exp(jax.random.uniform(key_cols, (1, FF), jnp.float32, 0.0, math.log(10.0)))
    common = jax.random.normal(key_common, (ROWS, FF), jnp.float32)
    own = jax.random.normal(key_own, (REPLICAS, ROWS, FF), jnp.float32)
    drift = 0.6 * common[None] + own
    return (start[None] + 0.02 * row_scale[None] * col_scale[None] * drift).astype(jnp.bfloat16)


def steps_of(own_key, dims, shards, low, top_value):
    loudness = 1.0
    for axis_at, parts in shards:
        steps = jax.random.uniform(jax.random.fold_in(jax.random.fold_in(own_key, 6), axis_at), (parts,), jnp.float32, low / len(shards), top_value / len(shards))
        loudness = loudness * jnp.repeat(jnp.exp(steps), dims[axis_at] // parts).reshape((-1,) + (1,) * (len(dims) - 1 - axis_at))
    return loudness


def centred(rng, extent, spread, limit, pieces=(), kind=jnp.bfloat16):
    entries = jax.random.normal(rng, extent, jnp.float32) * spread
    if len(pieces) > 0:
        entries = steps_of(rng, extent, pieces, -0.22, 0.18) * entries
    return jnp.clip(entries, min=-limit, max=limit).astype(kind)


def setup_inputs(seed: int = 0) -> dict:
    keys = jax.random.split(jax.random.key(seed), 4)
    return {
        "base": draw_base(jax.random.fold_in(keys[3], 71), 0),
        "local": draw_local(jax.random.fold_in(keys[3], 71), 0),
        "momentum": centred(keys[2], (ROWS, FF), 0.1, 0.6, ((0, 16), (1, 16)), jnp.float32),
    }


outer_rate = 0.7
momentum_decay = 0.9

def decoded(delta):
    blocks = delta.reshape(ROWS, FF // 128, 128)
    largest = lax.optimization_barrier(jnp.max(jnp.abs(blocks), axis=2))
    scale_low = ((largest + 1e-06) / 448.0).astype(jnp.bfloat16)
    scale = lax.optimization_barrier(scale_low).astype(jnp.float32)
    coded = (blocks / scale[:, :, None]).astype(jnp.bfloat16)
    return (coded.astype(jnp.float32) * scale[:, :, None]).reshape(ROWS, FF)

def reference(base, local, momentum):
    base_wide = base.astype(jnp.float32)

    def accumulate(index, total):
        replica_params = lax.dynamic_index_in_dim(local, index, 0, keepdims=False)
        return total + decoded(base_wide - replica_params.astype(jnp.float32))
    total = lax.fori_loop(0, REPLICAS, accumulate, jnp.zeros((ROWS, FF), jnp.float32))
    outer_grad = total / REPLICAS
    grad_rms = jnp.sqrt(jnp.sum(outer_grad * outer_grad) / (ROWS * FF))
    new_momentum = momentum_decay * momentum + outer_grad
    new_params = (base_wide - outer_rate * (momentum_decay * new_momentum + outer_grad)).astype(jnp.bfloat16)
    return (new_params, new_momentum, grad_rms)
```

```python
import functools

import jax
import jax.numpy as jnp
from jax import lax
from jax.experimental import pallas as pl
from jax.experimental.pallas import tpu as pltpu
from jax.sharding import PartitionSpec as P

MESH = pl.DeviceIdType.MESH
LANES = 128
SIDE = 4
outer_rate = 0.7
momentum_decay = 0.9

CHUNKS = ((0, 4, "x"), (11, 3, "z"), (4, 4, "x"), (8, 3, "x"))
ORDER = (
    ("e0", 0), ("e0", 1), ("e1", 0), ("e1", 1), ("e2", 0), ("e3", 0), ("e0", 2), ("e1", 2), ("e2", 1), ("e3", 1),
    ("r3", 0), ("e0", 3), ("e1", 3), ("e2", 2), ("e3", 2), ("e3", 3), ("r4", 0), ("r5", 0),
    ("r3", 1), ("r3", 2), ("e2", 3), ("r4", 1), ("g6", 0), ("r4", 2), ("r5", 1), ("g7", 0), ("r5", 2),
    ("r3", 3), ("g6", 1), ("r4", 3), ("g6", 2), ("g7", 1), ("r5", 3), ("n0", 0), ("g7", 2), ("g8", 0), ("g6", 3),
    ("n1", 0), ("g8", 1), ("g7", 3), ("n2", 0), ("g8", 2), ("n3", 0), ("g8", 3), ("g9", 0), ("g9", 1), ("g9", 2), ("g9", 3),
)


def kernel(
    base_hbm, local_hbm, momentum_hbm, params_ref, new_momentum_ref, rms_ref,
    base_ref, local_ref, momentum_ref, coded_ref,
    full_l, full_r, half_l, half_r, last_l, last_r, part_l, part_r,
    squares_ref, norm_ref, load_sem, send_sem, recv_sem,
):
    rows, columns = base_ref.shape
    half = rows // 2
    piece = columns // (SIDE * SIDE)
    replica = lax.axis_index("replica")
    fsdp = lax.axis_index("fsdp")
    at = {"x": replica // SIDE, "z": replica % SIDE}
    near, z_lo = fsdp % 2, fsdp // 8
    y = (fsdp // 2) % 4

    def shifted(axis, step):
        return (at[axis] + step + SIDE) % SIDE

    def device(axis, step):
        x, z = at["x"], at["z"]
        if axis == "x":
            x = shifted("x", step)
        else:
            z = shifted("z", step)
        return (x * SIDE + z, fsdp)

    def fsdp_device(axis, step):
        if axis == "y":
            return (replica, z_lo * 8 + (y + step) % 4 * 2 + near)
        other = (z_lo * 2 + near + step) % 4
        return (replica, other // 2 * 8 + y * 2 + other % 2)

    group = SIDE * piece
    loads = {}
    for i, step in enumerate((2, 1, -1, 0)):
        cols = pl.ds(pl.multiple_of(shifted("x", step) * group, LANES), group)
        loads[step] = (
            pltpu.make_async_copy(base_hbm.at[:, cols], base_ref.at[:, cols], load_sem.at[2 * i]),
            pltpu.make_async_copy(local_hbm.at[0, :, cols], local_ref.at[:, cols], load_sem.at[2 * i + 1]),
        )
        for copy in loads[step]:
            copy.start()
    momentum_load = pltpu.make_async_copy(momentum_hbm, momentum_ref, load_sem.at[8])
    momentum_load.start()
    squares_ref[...] = jnp.zeros_like(squares_ref)

    barrier = pltpu.get_barrier_semaphore()
    peers = [device(axis, step) for axis in ("x", "z") for step in (1, 2, 3)]
    peers += [fsdp_device(axis, step) for axis in ("y", "other") for step in (1, 2, 3)]
    for peer in peers:
        pl.semaphore_signal(barrier, inc=1, device_id=peer, device_id_type=MESH)
    entered = []
    waited = set()

    def loaded(step):
        if step not in waited:
            waited.add(step)
            for copy in loads[step]:
                copy.wait()

    copies = {}

    def send(key, src, dst, target):
        if not entered:
            entered.append(True)
            pl.semaphore_wait(barrier, len(peers))
        i = len(copies)
        copy = pltpu.make_async_remote_copy(
            src_ref=src, dst_ref=dst, send_sem=send_sem.at[i], recv_sem=recv_sem.at[i],
            device_id=target, device_id_type=MESH,
        )
        copy.start()
        copies[key] = copy

    def recv(*key):
        copies[key].wait_recv()

    low, high, every = pl.ds(0, half), pl.ds(half, half), pl.ds(0, rows)

    def column(x, z, block):
        return pl.multiple_of((x * SIDE + z) * piece + block * LANES, LANES)

    def code_block(block, x, z):
        cols = pl.ds(column(x, z, block), LANES)
        delta = base_ref[:, cols].astype(jnp.float32) - local_ref[:, cols].astype(jnp.float32)
        largest = jnp.max(jnp.abs(delta), axis=1, keepdims=True)
        scale = ((largest + 1e-06) * (1.0 / 448.0)).astype(jnp.bfloat16).astype(jnp.float32)
        coded = (delta / scale).astype(jnp.bfloat16).astype(jnp.float32)
        coded_ref[block, x, z] = (coded * scale).astype(jnp.bfloat16)

    def over(start, count, body, unroll=2):
        def step(i, carry):
            body(start + i // SIDE, i % SIDE)
            return carry
        lax.fori_loop(0, count * SIDE, step, 0, unroll=unroll)

    def blocks(start, count, body):
        def step(i, carry):
            body(start + i)
            return carry
        lax.fori_loop(0, count, step, 0)

    def f32(value):
        return value.astype(jnp.float32)

    steps = {}
    for c, (start, count, first) in enumerate(CHUNKS):
        second = "z" if first == "x" else "x"
        ks = pl.ds(start, count)

        def xz(f, s, first=first):
            return (f, s) if first == "x" else (s, f)

        def row_of(f, rs, ks=ks, first=first):
            if first == "x":
                return coded_ref.at[ks, f, :, rs]
            return coded_ref.at[ks, :, f, rs]

        def piece_of(f, s, rs, ks=ks, xz=xz):
            return coded_ref.at[(ks, *xz(f, s), rs)]

        def gathered(f, s, rs, start=start, count=count, xz=xz):
            return params_ref.at[rs, pl.ds(column(*xz(f, s), start), count * LANES)]

        def code(f_step, start=start, count=count, first=first, xz=xz):
            if first == "x":
                loaded(f_step)
            else:
                for step in (2, 1, -1, 0):
                    loaded(step)
            f = shifted(first, f_step)
            over(start, count, lambda block, s: code_block(block, *xz(f, s)))

        def e0(c=c, ks=ks, first=first, row_of=row_of, code=code):
            code(2)
            far = shifted(first, 2)
            send(("p_r", c), row_of(far, low), half_l.at[ks], device(first, 1))
            send(("p_l", c), row_of(far, high), half_r.at[ks], device(first, -1))

        def e1(c=c, ks=ks, first=first, row_of=row_of, code=code):
            code(1)
            send(("w_r", c), row_of(shifted(first, 1), high), full_l.at[ks, :, high], device(first, 1))
            code(-1)
            send(("w_l", c), row_of(shifted(first, -1), low), full_r.at[ks, :, low], device(first, -1))

        def e2(c=c, ks=ks, start=start, count=count, first=first, row_of=row_of, xz=xz):
            for name, step, rs, got, into in (
                ("r", 1, low, half_l, full_l), ("l", -1, high, half_r, full_r),
            ):
                f = shifted(first, step)
                recv("p_" + name, c)

                def add(block, s, f=f, rs=rs, got=got):
                    index = (block, *xz(f, s), rs)
                    coded_ref[index] = (f32(coded_ref[index]) + f32(got[block, s])).astype(jnp.bfloat16)
                over(start, count, add)
                send(("s_" + name, c), row_of(f, rs), into.at[ks, :, rs], device(first, step))

        def e3(code=code):
            code(0)

        def r3(c=c, ks=ks, start=start, count=count, first=first, second=second, piece_of=piece_of, xz=xz):
            for name in ("w_r", "w_l", "s_r", "s_l"):
                recv(name, c)
            f = at[first]

            def add(block, s):
                index = (block, *xz(f, s))
                total = f32(coded_ref[index]) + f32(full_l[block, s]) + f32(full_r[block, s])
                coded_ref[index] = total.astype(jnp.bfloat16)
            over(start, count, add)
            far = shifted(second, 2)
            send(("P_r", c), piece_of(f, far, low), part_l.at[ks], device(second, 1))
            send(("P_l", c), piece_of(f, far, high), part_r.at[ks], device(second, -1))
            send(("W_r", c), piece_of(f, shifted(second, 1), high), last_l.at[ks, high], device(second, 1))
            send(("W_l", c), piece_of(f, shifted(second, -1), low), last_r.at[ks, low], device(second, -1))

        def r4(c=c, ks=ks, start=start, count=count, first=first, second=second, piece_of=piece_of, xz=xz):
            f = at[first]
            for name, step, rs, got, into in (
                ("r", 1, low, part_l, last_l), ("l", -1, high, part_r, last_r),
            ):
                s = shifted(second, step)
                recv("P_" + name, c)

                def add(block, s=s, rs=rs, got=got):
                    index = (block, *xz(f, s), rs)
                    coded_ref[index] = (f32(coded_ref[index]) + f32(got[block])).astype(jnp.bfloat16)
                blocks(start, count, add)
                send(("S_" + name, c), piece_of(f, s, rs), into.at[ks, rs], device(second, step))

        def spread(c, first, gathered, s):
            for name, step in (("r", 1), ("l", -1)):
                part = gathered(at[first], shifted(second_of[first], s), every)
                send(("G_" + name, s, c), part, part, device(first, step))

        def r5(c=c, start=start, count=count, first=first, second=second, gathered=gathered, spread=spread):
            for name in ("W_r", "W_l", "S_r", "S_l"):
                recv(name, c)
            if "momentum" not in waited:
                waited.add("momentum")
                momentum_load.wait()

            def update(block):
                x, z = at["x"], at["z"]
                total = f32(coded_ref[block, x, z]) + f32(last_l[block]) + f32(last_r[block])
                grad = total * (1.0 / (SIDE * SIDE))
                squares_ref[...] += jnp.sum((grad * grad).reshape(rows // 8, 8, LANES), axis=0)
                own = pl.ds(pl.multiple_of(block * LANES, LANES), LANES)
                new_momentum = momentum_decay * momentum_ref[:, own] + grad
                new_momentum_ref[:, own] = new_momentum
                cols = pl.ds(column(x, z, block), LANES)
                stepped = f32(base_ref[:, cols]) - outer_rate * (momentum_decay * new_momentum + grad)
                params_ref[:, cols] = stepped.astype(jnp.bfloat16)
            blocks(start, count, update)
            mine = gathered(at[first], at[second], every)
            send(("g_r", c), mine, mine, device(second, 1))
            send(("g_l", c), mine, mine, device(second, -1))
            spread(c, first, gathered, 0)

        def g6(c=c, first=first, second=second, gathered=gathered, spread=spread):
            for name, step, rs in (("r", 1, low), ("l", -1, high)):
                recv("g_" + name, c)
                passed = gathered(at[first], shifted(second, -step), rs)
                send(("h_" + name, c), passed, passed, device(second, step))
            spread(c, first, gathered, 1)
            spread(c, first, gathered, -1)

        def g7(c=c, first=first, gathered=gathered, spread=spread):
            recv("h_r", c)
            recv("h_l", c)
            spread(c, first, gathered, 2)

        def g8(c=c, first=first, second=second, gathered=gathered):
            for s in (0, 1, -1, 2):
                for name, step, rs in (("r", 1, low), ("l", -1, high)):
                    recv("G_" + name, s, c)
                    passed = gathered(shifted(first, -step), shifted(second, s), rs)
                    send(("H_" + name, s, c), passed, passed, device(first, step))

        def g9(c=c):
            for s in (0, 1, -1, 2):
                recv("H_r", s, c)
                recv("H_l", s, c)

        for step in (e0, e1, e2, e3, r3, r4, r5, g6, g7, g8, g9):
            steps[step.__name__, c] = step

    def norm_round(i, place, target):
        for step in (1, 2, 3):
            send(("n", i, step), norm_ref.at[i, place], norm_ref.at[i, place], target(step))

    def norm_sum(i):
        for step in (1, 2, 3):
            recv("n", i, step)
        return norm_ref[i, 0] + norm_ref[i, 1] + norm_ref[i, 2] + norm_ref[i, 3]

    other = z_lo * 2 + near

    def n0():
        norm_ref[0, at["x"]] = squares_ref[...]
        norm_round(0, at["x"], lambda step: device("x", step))

    def n1():
        norm_ref[1, at["z"]] = norm_sum(0)
        norm_round(1, at["z"], lambda step: device("z", step))

    def n2():
        norm_ref[2, y] = norm_sum(1)
        norm_round(2, y, lambda step: fsdp_device("y", step))

    def n3():
        norm_ref[3, other] = norm_sum(2)
        norm_round(3, other, lambda step: fsdp_device("other", step))

    for step in (n0, n1, n2, n3):
        steps[step.__name__, 0] = step

    for key in ORDER:
        steps[key]()
    total = jnp.sum(norm_sum(3), axis=(0, 1), keepdims=True)
    entries = rows * columns * 16
    rms_ref[...] = jnp.broadcast_to(jnp.sqrt(total / entries), rms_ref.shape)
    for copy in copies.values():
        copy.wait_send()


second_of = {"x": "z", "z": "x"}
COPIES = len(CHUNKS) * (4 + 2 + 2 + 4 + 8 + 8 + 4) + 12


def per_device(base, local, momentum):
    rows, columns = base.shape
    piece = columns // (SIDE * SIDE)
    number = piece // LANES
    half = rows // 2
    bf16 = functools.partial(pltpu.VMEM, dtype=jnp.bfloat16)
    vmem = pl.BlockSpec(memory_space=pltpu.VMEM)
    new_params, new_momentum, rms = pl.pallas_call(
        kernel,
        out_shape=(
            pltpu.VMEM((rows, columns), jnp.bfloat16),
            pltpu.VMEM((rows, piece), jnp.float32),
            pltpu.VMEM((8, LANES), jnp.float32),
        ),
        in_specs=[pl.BlockSpec(memory_space=pltpu.HBM)] * 3,
        out_specs=(vmem, vmem, vmem),
        scratch_shapes=[
            bf16((rows, columns)),
            bf16((rows, columns)),
            pltpu.VMEM((rows, piece), jnp.float32),
            bf16((number, SIDE, SIDE, rows, LANES)),
            bf16((number, SIDE, rows, LANES)),
            bf16((number, SIDE, rows, LANES)),
            bf16((number, SIDE, half, LANES)),
            bf16((number, SIDE, half, LANES)),
            bf16((number, rows, LANES)),
            bf16((number, rows, LANES)),
            bf16((number, half, LANES)),
            bf16((number, half, LANES)),
            pltpu.VMEM((8, LANES), jnp.float32),
            pltpu.VMEM((4, 4, 8, LANES), jnp.float32),
            pltpu.SemaphoreType.DMA((9,)),
            pltpu.SemaphoreType.DMA((COPIES,)),
            pltpu.SemaphoreType.DMA((COPIES,)),
        ],
        compiler_params=pltpu.CompilerParams(
            collective_id=0, has_side_effects=True, vmem_limit_bytes=40 * 2**20
        ),
        name="outer_step",
    )(*(pltpu.with_memory_space_constraint(a, pltpu.HBM) for a in (base, local, momentum)))
    return (new_params, new_momentum, rms[0, 0])


def solution(mesh):
    return jax.shard_map(
        per_device,
        mesh=mesh,
        in_specs=(P("fsdp", None), P("replica", "fsdp", None), P("fsdp", "replica")),
        out_specs=(P("fsdp", None), P("fsdp", "replica"), P()),
        check_vma=False,
    )
```

```python
import functools

import jax
import jax.numpy as jnp
from jax import lax
from jax.experimental import pallas as pl
from jax.experimental.pallas import tpu as pltpu
from jax.sharding import PartitionSpec as P

MESH = pl.DeviceIdType.MESH
LANES = 128
SIDE = 4
outer_rate = 0.7
momentum_decay = 0.9

CHUNKS = (
    (0, 2, "x"),
    (11, 1, "z"),
    (2, 2, "x"),
    (12, 1, "z"),
    (4, 2, "x"),
    (13, 1, "z"),
    (6, 2, "x"),
    (8, 2, "x"),
    (10, 1, "x"),
)
ORDER = (
    ("E2", 2), ("Sp", 2), ("E2", 5), ("E2", 1), ("Sp", 5), ("E2", 0), ("Sp", 0), ("Sp", 1), ("E1l", 2), ("E1r", 0), ("Swr", 0), ("Swl", 2), ("E2", 3),
    ("E1l", 5), ("E1l", 0), ("E1r", 2), ("Swl", 5), ("Swl", 0), ("Sp", 3), ("Swr", 2), ("A2r", 2), ("E1r", 5), ("E1l", 1), ("E1l", 8), ("A2l", 2),
    ("A2r", 0), ("Swr", 5), ("E1r", 1), ("A2l", 0), ("Swl", 8), ("A2r", 5), ("A2l", 5), ("E2", 7), ("A2l", 1), ("E2", 4), ("E2", 8), ("Sp", 8),
    ("E1r", 8), ("A2r", 1), ("Sp", 4), ("E1l", 4), ("E2", 6), ("Swr", 8), ("E0", 2), ("R3a", 2), ("E1l", 3), ("Swl", 1), ("Sp", 6), ("Swr", 1),
    ("E0", 3), ("E0", 0), ("E1l", 6), ("Sp", 7), ("R3a", 0), ("E1r", 4), ("A2r", 8), ("R3b", 2), ("A2l", 8), ("E0", 5), ("R3b", 0), ("Swl", 4),
    ("R3c", 2), ("Swr", 4), ("E1r", 6), ("R4r", 2), ("R4l", 2), ("A2l", 4), ("A2l", 3), ("E1r", 3), ("Swr", 3), ("E1r", 7), ("Swl", 6), ("A2r", 4),
    ("E0", 4), ("A2l", 6), ("R4r", 0), ("R4l", 0), ("Swr", 6), ("Swl", 3), ("A2r", 6), ("A2r", 3), ("A2r", 7), ("Swr", 7), ("E1l", 7), ("E0", 8),
    ("R3a", 8), ("Swl", 7), ("R3b", 8), ("R3c", 0), ("A2l", 7), ("R5", 2), ("R3a", 5), ("E0", 6), ("R3a", 4), ("R5", 0), ("R3b", 4), ("R3a", 3),
    ("E0", 7), ("R3c", 3), ("R3a", 6), ("R4l", 8), ("R3c", 4), ("R4r", 8), ("R3c", 8), ("E0", 1), ("G6r", 2), ("G6l", 2), ("R3b", 6), ("R4l", 4),
    ("R4r", 4), ("R3a", 7), ("R3a", 1), ("R3b", 5), ("R4r", 5), ("R4l", 5), ("G6l", 0), ("G6r", 0), ("R3c", 6), ("R3c", 5), ("R4r", 6), ("R4l", 6),
    ("R3b", 3), ("R5", 8), ("R3b", 7), ("G8l", 2, 0), ("R3c", 7), ("R4r", 3), ("R3b", 1), ("G8l", 2, -1), ("R5", 5), ("G7", 2), ("R4r", 7),
    ("R4l", 7), ("R4l", 3), ("R4l", 1), ("G8r", 2, 1), ("R4r", 1), ("G8l", 0, 1), ("R5", 4), ("G8r", 0, 0), ("G6r", 8), ("R3c", 1), ("G6l", 8),
    ("R5", 6), ("R5", 3), ("G7", 0), ("R5", 7), ("R5", 1), ("N0", 0), ("G8r", 0, -1), ("G8l", 0, 0), ("G8l", 4, 0), ("G8r", 0, 1), ("G6l", 4),
    ("G6r", 4), ("G8r", 8, 1), ("G8l", 2, 1), ("G6l", 3), ("G6r", 3), ("G8l", 0, -1), ("G6r", 6), ("G7", 8), ("G8l", 0, 2), ("G8r", 2, 0), ("G6r", 1),
    ("G6l", 1), ("G6r", 7), ("G8r", 2, -1), ("G8r", 6, 0), ("G6r", 5), ("G6l", 7), ("G8r", 4, -1), ("G8r", 8, -1), ("G6l", 5), ("N1", 0), ("G7", 4),
    ("G6l", 6), ("G8l", 2, 2), ("G8l", 4, -1), ("G8r", 4, 0), ("G8l", 3, 0), ("G7", 1), ("G8r", 7, 0), ("G7", 3), ("G8r", 4, 1), ("G8l", 6, 0),
    ("G8l", 6, -1), ("G8r", 0, 2), ("G8r", 8, 2), ("G8l", 4, 1), ("G7", 5), ("G8l", 7, 0), ("G8r", 3, 0), ("G8l", 3, -1), ("G7", 7), ("G8r", 3, -1),
    ("G8l", 5, -1), ("N2", 0), ("G8l", 8, 1), ("G8l", 1, -1), ("G8r", 3, 1), ("G8l", 8, 0), ("G8r", 5, -1), ("G8l", 1, 1), ("G8r", 6, -1), ("G7", 6),
    ("G8r", 1, 0), ("G8l", 8, 2), ("G8r", 7, 1), ("G8r", 1, -1), ("G8r", 5, 0), ("G8l", 5, 1), ("G8l", 3, 1), ("G8r", 4, 2), ("G8r", 1, 2),
    ("G8l", 7, -1), ("G8r", 1, 1), ("G8r", 7, -1), ("G8r", 2, 2), ("N3", 0), ("G8r", 3, 2), ("G8l", 1, 0), ("G8l", 4, 2), ("G8l", 6, 1),
    ("G8l", 1, 2), ("G8l", 3, 2), ("G8r", 6, 1), ("G8r", 5, 2), ("G8r", 8, 0), ("G8l", 8, -1), ("G8r", 7, 2), ("G8l", 7, 2), ("G8r", 5, 1),
    ("G8l", 5, 2), ("G8l", 5, 0), ("G8l", 7, 1), ("G8r", 6, 2), ("G8l", 6, 2), ("G9", 0), ("G9", 2), ("G9", 4), ("G9", 8), ("G9", 1), ("G9", 7),
    ("G9", 3), ("G9", 6), ("G9", 5),
)


def kernel(
    base_hbm, local_hbm, momentum_hbm, params_ref, new_momentum_ref, rms_ref,
    base_ref, local_ref, momentum_ref, coded_ref,
    full_l, full_r, half_l, half_r, last_l, last_r, part_l, part_r,
    squares_ref, norm_ref, load_sem, send_sem, recv_sem,
):
    rows, columns = base_ref.shape
    half = rows // 2
    piece = columns // (SIDE * SIDE)
    replica = lax.axis_index("replica")
    fsdp = lax.axis_index("fsdp")
    at = {"x": replica // SIDE, "z": replica % SIDE}
    near, z_lo = fsdp % 2, fsdp // 8
    y = (fsdp // 2) % 4

    def shifted(axis, step):
        return (at[axis] + step + SIDE) % SIDE

    def device(axis, step):
        x, z = at["x"], at["z"]
        if axis == "x":
            x = shifted("x", step)
        else:
            z = shifted("z", step)
        return (x * SIDE + z, fsdp)

    def fsdp_device(axis, step):
        if axis == "y":
            return (replica, z_lo * 8 + (y + step) % 4 * 2 + near)
        other = (z_lo * 2 + near + step) % 4
        return (replica, other // 2 * 8 + y * 2 + other % 2)

    group = SIDE * piece
    loads = {}
    for i, step in enumerate((2, 1, -1, 0)):
        cols = pl.ds(pl.multiple_of(shifted("x", step) * group, LANES), group)
        loads[step] = (
            pltpu.make_async_copy(base_hbm.at[:, cols], base_ref.at[:, cols], load_sem.at[2 * i]),
            pltpu.make_async_copy(local_hbm.at[0, :, cols], local_ref.at[:, cols], load_sem.at[2 * i + 1]),
        )
        for copy in loads[step]:
            copy.start()
    momentum_load = pltpu.make_async_copy(momentum_hbm, momentum_ref, load_sem.at[8])
    momentum_load.start()
    squares_ref[...] = jnp.zeros_like(squares_ref)

    barrier = pltpu.get_barrier_semaphore()
    peers = [device(axis, step) for axis in ("x", "z") for step in (1, 2, 3)]
    peers += [fsdp_device(axis, step) for axis in ("y", "other") for step in (1, 2, 3)]
    for peer in peers:
        pl.semaphore_signal(barrier, inc=1, device_id=peer, device_id_type=MESH)
    entered = []
    waited = set()

    def loaded(step):
        if step not in waited:
            waited.add(step)
            for copy in loads[step]:
                copy.wait()

    groups = {}

    def send(key, src, dst, target):
        if not entered:
            entered.append(True)
            pl.semaphore_wait(barrier, len(peers))
        together = (GROUP[key[0]], key[-1]) if key[0] in GROUP else key
        i = groups.setdefault(together, len(groups))
        pltpu.make_async_remote_copy(
            src_ref=src, dst_ref=dst, send_sem=send_sem.at[key[-1]], recv_sem=recv_sem.at[i],
            device_id=target, device_id_type=MESH,
        ).start()

    def wait(sem, sized):
        pltpu.make_async_copy(sized, sized, sem).wait()

    def recv(key, sized):
        wait(recv_sem.at[groups[key]], sized)

    def pieces(count, x, z, rs=slice(None)):
        return coded_ref.at[pl.ds(0, count), pl.ds(0, x), pl.ds(0, z), rs]

    low, high, every = pl.ds(0, half), pl.ds(half, half), pl.ds(0, rows)

    def column(x, z, block):
        return pl.multiple_of((x * SIDE + z) * piece + block * LANES, LANES)

    def code_block(block, x, z):
        cols = pl.ds(column(x, z, block), LANES)
        delta = base_ref[:, cols].astype(jnp.float32) - local_ref[:, cols].astype(jnp.float32)
        largest = jnp.max(jnp.abs(delta), axis=1, keepdims=True)
        scale = ((largest + 1e-06) * (1.0 / 448.0)).astype(jnp.bfloat16).astype(jnp.float32)
        coded = (delta / scale).astype(jnp.bfloat16).astype(jnp.float32)
        coded_ref[block, x, z] = (coded * scale).astype(jnp.bfloat16)

    def over(start, count, body, unroll=2):
        def step(i, carry):
            body(start + i // SIDE, i % SIDE)
            return carry
        lax.fori_loop(0, count * SIDE, step, 0, unroll=unroll)

    def blocks(start, count, body):
        def step(i, carry):
            body(start + i)
            return carry
        lax.fori_loop(0, count, step, 0)

    def f32(value):
        return value.astype(jnp.float32)

    steps = {}
    for c, (start, count, first) in enumerate(CHUNKS):
        second = "z" if first == "x" else "x"
        ks = pl.ds(start, count)

        def xz(f, s, first=first):
            return (f, s) if first == "x" else (s, f)

        def row_of(f, rs, ks=ks, first=first):
            if first == "x":
                return coded_ref.at[ks, f, :, rs]
            return coded_ref.at[ks, :, f, rs]

        def piece_of(f, s, rs, ks=ks, xz=xz):
            return coded_ref.at[(ks, *xz(f, s), rs)]

        def gathered(f, s, rs, start=start, count=count, xz=xz):
            return params_ref.at[rs, pl.ds(column(*xz(f, s), start), count * LANES)]

        def code(f_step, start=start, count=count, first=first, xz=xz):
            if first == "x":
                loaded(f_step)
            else:
                for step in (2, 1, -1, 0):
                    loaded(step)
            f = shifted(first, f_step)
            over(start, count, lambda block, s: code_block(block, *xz(f, s)))


        def E2(code=code):
            code(2)

        def E1r(code=code):
            code(1)

        def E1l(code=code):
            code(-1)

        def E0(code=code):
            code(0)

        def Sp(c=c, ks=ks, first=first, row_of=row_of):
            far = shifted(first, 2)
            send(("p_r", c), row_of(far, low), half_l.at[ks], device(first, 1))
            send(("p_l", c), row_of(far, high), half_r.at[ks], device(first, -1))

        def Swr(c=c, ks=ks, first=first, row_of=row_of):
            send(("w_r", c), row_of(shifted(first, 1), high), full_l.at[ks, :, high], device(first, 1))

        def Swl(c=c, ks=ks, first=first, row_of=row_of):
            send(("w_l", c), row_of(shifted(first, -1), low), full_r.at[ks, :, low], device(first, -1))

        def join(name, step, rs, got, into, c=c, ks=ks, start=start, count=count, first=first, row_of=row_of, xz=xz):
            f = shifted(first, step)
            recv(("p_" + name, c), pieces(count, 4, 1, low))

            def add(block, s):
                index = (block, *xz(f, s), rs)
                coded_ref[index] = (f32(coded_ref[index]) + f32(got[block, s])).astype(jnp.bfloat16)
            over(start, count, add)
            send(("s_" + name, c), row_of(f, rs), into.at[ks, :, rs], device(first, step))

        def A2r(join=join):
            join("r", 1, low, half_l, full_l)

        def A2l(join=join):
            join("l", -1, high, half_r, full_r)

        def total_at(s, start=start, count=count, first=first, xz=xz):
            def add(block):
                index = (block, *xz(at[first], s))
                total = f32(coded_ref[index]) + f32(full_l[block, s]) + f32(full_r[block, s])
                coded_ref[index] = total.astype(jnp.bfloat16)
            blocks(start, count, add)

        def R3a(c=c, ks=ks, count=count, first=first, second=second, piece_of=piece_of, total_at=total_at):
            recv(("first", c), pieces(count, 4, 2))
            far = shifted(second, 2)
            total_at(far)
            send(("P_r", c), piece_of(at[first], far, low), part_l.at[ks], device(second, 1))
            send(("P_l", c), piece_of(at[first], far, high), part_r.at[ks], device(second, -1))

        def R3b(c=c, ks=ks, first=first, second=second, piece_of=piece_of, total_at=total_at):
            for name, step, rs, into in (("r", 1, high, last_l), ("l", -1, low, last_r)):
                s = shifted(second, step)
                total_at(s)
                send(("W_" + name, c), piece_of(at[first], s, rs), into.at[ks, rs], device(second, step))

        def R3c(second=second, total_at=total_at):
            total_at(at[second])

        def last_join(name, step, rs, got, into, c=c, ks=ks, start=start, count=count, first=first, second=second,
                      piece_of=piece_of, xz=xz):
            s = shifted(second, step)
            recv(("P_" + name, c), pieces(count, 1, 1, low))

            def add(block):
                index = (block, *xz(at[first], s), rs)
                coded_ref[index] = (f32(coded_ref[index]) + f32(got[block])).astype(jnp.bfloat16)
            blocks(start, count, add)
            send(("S_" + name, c), piece_of(at[first], s, rs), into.at[ks, rs], device(second, step))

        def R4r(last_join=last_join):
            last_join("r", 1, low, part_l, last_l)

        def R4l(last_join=last_join):
            last_join("l", -1, high, part_r, last_r)

        def spread(s, c=c, first=first, second=second, gathered=gathered):
            for name, step in (("r", 1), ("l", -1)):
                part = gathered(at[first], shifted(second, s), every)
                send(("G_" + name, s, c), part, part, device(first, step))

        def R5(c=c, start=start, count=count, first=first, second=second, gathered=gathered, spread=spread):
            recv(("second", c), pieces(count, 1, 2))
            if "momentum" not in waited:
                waited.add("momentum")
                momentum_load.wait()

            def update(block):
                x, z = at["x"], at["z"]
                total = f32(coded_ref[block, x, z]) + f32(last_l[block]) + f32(last_r[block])
                grad = total * (1.0 / (SIDE * SIDE))
                squares_ref[...] += jnp.sum((grad * grad).reshape(rows // 8, 8, LANES), axis=0)
                own = pl.ds(pl.multiple_of(block * LANES, LANES), LANES)
                new_momentum = momentum_decay * momentum_ref[:, own] + grad
                new_momentum_ref[:, own] = new_momentum
                cols = pl.ds(column(x, z, block), LANES)
                stepped = f32(base_ref[:, cols]) - outer_rate * (momentum_decay * new_momentum + grad)
                params_ref[:, cols] = stepped.astype(jnp.bfloat16)
            blocks(start, count, update)
            mine = gathered(at[first], at[second], every)
            send(("g_r", c), mine, mine, device(second, 1))
            send(("g_l", c), mine, mine, device(second, -1))
            spread(0)

        def pass_on(name, step, rs, c=c, count=count, first=first, second=second, gathered=gathered, spread=spread):
            recv(("g_" + name, c), pieces(count, 1, 1))
            passed = gathered(at[first], shifted(second, -step), rs)
            send(("h_" + name, c), passed, passed, device(second, step))
            spread(-step)

        def G6r(pass_on=pass_on):
            pass_on("r", 1, low)

        def G6l(pass_on=pass_on):
            pass_on("l", -1, high)

        def G7(c=c, count=count, spread=spread):
            recv(("far", c), pieces(count, 1, 1))
            spread(2)

        def last_pass(s, name, step, rs, c=c, count=count, first=first, second=second, gathered=gathered):
            recv(("G_" + name, s, c), pieces(count, 1, 1))
            passed = gathered(shifted(first, -step), shifted(second, s), rs)
            send(("H_" + name, s, c), passed, passed, device(first, step))

        def G9(c=c, count=count):
            recv(("last", c), pieces(count, 4, 1))

        for step in (E2, E1r, E1l, E0, Sp, Swr, Swl, A2r, A2l, R3a, R3b, R3c, R4r, R4l, R5, G6r, G6l, G7, G9):
            steps[step.__name__, c] = step
        for s in (0, 1, -1, 2):
            steps["G8r", c, s] = functools.partial(last_pass, s, "r", 1, low)
            steps["G8l", c, s] = functools.partial(last_pass, s, "l", -1, high)

    def norm_round(i, place, target):
        for step in (1, 2, 3):
            send((f"n{i}", len(CHUNKS)), norm_ref.at[i, place], norm_ref.at[i, place], target(step))

    def norm_sum(i):
        recv((f"n{i}", len(CHUNKS)), norm_ref.at[0, pl.ds(0, 3)])
        return norm_ref[i, 0] + norm_ref[i, 1] + norm_ref[i, 2] + norm_ref[i, 3]

    other = z_lo * 2 + near

    def N0():
        norm_ref[0, at["x"]] = squares_ref[...]
        norm_round(0, at["x"], lambda step: device("x", step))

    def N1():
        norm_ref[1, at["z"]] = norm_sum(0)
        norm_round(1, at["z"], lambda step: device("z", step))

    def N2():
        norm_ref[2, y] = norm_sum(1)
        norm_round(2, y, lambda step: fsdp_device("y", step))

    def N3():
        norm_ref[3, other] = norm_sum(2)
        norm_round(3, other, lambda step: fsdp_device("other", step))

    for step in (N0, N1, N2, N3):
        steps[step.__name__, 0] = step

    for key in ORDER:
        steps[key]()
    total = jnp.sum(norm_sum(3), axis=(0, 1), keepdims=True)
    entries = rows * columns * 16
    rms_ref[...] = jnp.broadcast_to(jnp.sqrt(total / entries), rms_ref.shape)
    for c, (_, count, _) in enumerate(CHUNKS):
        wide, high_, deep = SENT[count]
        wait(send_sem.at[c], coded_ref.at[pl.ds(0, wide), pl.ds(0, high_), pl.ds(0, deep)])
    wait(send_sem.at[len(CHUNKS)], norm_ref.at[pl.ds(0, 3)])


second_of = {"x": "z", "z": "x"}
SPLIT = 1
RECEIVES = len(CHUNKS) * 18 + 4
GROUP = {
    "w_r": "first", "w_l": "first", "s_r": "first", "s_l": "first",
    "W_r": "second", "W_l": "second", "S_r": "second", "S_l": "second",
    "h_r": "far", "h_l": "far", "H_r": "last", "H_l": "last",
}
SENT = {1: (10, 3, 1), 2: (5, 4, 3), 3: (10, 3, 3), 4: (10, 4, 3)}


def write_out(params_ref, momentum_ref, rms_ref, params_hbm, momentum_hbm, rms_hbm, sem):
    copies = [pltpu.make_async_copy(rms_ref, rms_hbm, sem.at[0])]
    for src, dst in ((params_ref, params_hbm), (momentum_ref, momentum_hbm)):
        step = src.shape[0] // SPLIT
        for i in range(SPLIT):
            part = pl.ds(i * step, step)
            copies.append(pltpu.make_async_copy(src.at[part], dst.at[part], sem.at[len(copies)]))
    for copy in copies:
        copy.start()
    for copy in copies:
        copy.wait()


def per_device(base, local, momentum):
    rows, columns = base.shape
    piece = columns // (SIDE * SIDE)
    number = piece // LANES
    half = rows // 2
    bf16 = functools.partial(pltpu.VMEM, dtype=jnp.bfloat16)
    vmem = pl.BlockSpec(memory_space=pltpu.VMEM)
    new_params, new_momentum, rms = pl.pallas_call(
        kernel,
        out_shape=(
            pltpu.VMEM((rows, columns), jnp.bfloat16),
            pltpu.VMEM((rows, piece), jnp.float32),
            pltpu.VMEM((1, 1), jnp.float32),
        ),
        in_specs=[pl.BlockSpec(memory_space=pltpu.HBM)] * 3,
        out_specs=(vmem, vmem, vmem),
        scratch_shapes=[
            bf16((rows, columns)),
            bf16((rows, columns)),
            pltpu.VMEM((rows, piece), jnp.float32),
            bf16((number, SIDE, SIDE, rows, LANES)),
            bf16((number, SIDE, rows, LANES)),
            bf16((number, SIDE, rows, LANES)),
            bf16((number, SIDE, half, LANES)),
            bf16((number, SIDE, half, LANES)),
            bf16((number, rows, LANES)),
            bf16((number, rows, LANES)),
            bf16((number, half, LANES)),
            bf16((number, half, LANES)),
            pltpu.VMEM((8, LANES), jnp.float32),
            pltpu.VMEM((4, 4, 8, LANES), jnp.float32),
            pltpu.SemaphoreType.DMA((9,)),
            pltpu.SemaphoreType.DMA((len(CHUNKS) + 1,)),
            pltpu.SemaphoreType.DMA((RECEIVES,)),
        ],
        compiler_params=pltpu.CompilerParams(
            collective_id=0, has_side_effects=True, vmem_limit_bytes=24 * 2**20
        ),
        name="outer_step",
    )(*(pltpu.with_memory_space_constraint(a, pltpu.HBM) for a in (base, local, momentum)))
    hbm = pl.BlockSpec(memory_space=pltpu.HBM)
    new_params, new_momentum, rms = pl.pallas_call(
        write_out,
        out_shape=(
            pltpu.HBM((rows, columns), jnp.bfloat16),
            pltpu.HBM((rows, piece), jnp.float32),
            pltpu.HBM((1, 1), jnp.float32),
        ),
        in_specs=[vmem] * 3,
        out_specs=(hbm,) * 3,
        scratch_shapes=[pltpu.SemaphoreType.DMA((2 * SPLIT + 1,))],
        compiler_params=pltpu.CompilerParams(vmem_limit_bytes=2**20),
        name="write_out",
    )(*(pltpu.with_memory_space_constraint(a, pltpu.VMEM) for a in (new_params, new_momentum, rms)))
    return (new_params, new_momentum, rms[0, 0])


def solution(mesh):
    return jax.shard_map(
        per_device,
        mesh=mesh,
        in_specs=(P("fsdp", None), P("replica", "fsdp", None), P("fsdp", "replica")),
        out_specs=(P("fsdp", None), P("fsdp", "replica"), P()),
        check_vma=False,
    )
```

```python
import functools

import jax
import jax.numpy as jnp
from jax import lax
from jax.experimental import pallas as pl
from jax.experimental.pallas import tpu as pltpu
from jax.sharding import PartitionSpec as P

MESH = pl.DeviceIdType.MESH
LANES = 128
SIDE = 4
outer_rate = 0.7
momentum_decay = 0.9

CHUNKS = (
    (0, 2, "x"),
    (11, 1, "z"),
    (2, 2, "x"),
    (12, 1, "z"),
    (4, 2, "x"),
    (13, 1, "z"),
    (6, 2, "x"),
    (8, 2, "x"),
    (10, 1, "x"),
)
ORDER = (
    ("E2", 0), ("Sp", 0), ("E2", 1), ("E2", 6), ("E2", 4), ("Sp", 1), ("Sp", 4), ("Sp", 6), ("E1l", 4), ("E1r", 4), ("E2", 5), ("Swl", 4), ("Swr", 4),
    ("Sp", 5), ("E2", 3), ("E2", 2), ("E1r", 3), ("E2", 8), ("Sp", 2), ("Sp", 3), ("E1l", 1), ("E1r", 1), ("Swl", 1), ("Swr", 3), ("E0", 4),
    ("Swr", 1), ("E1l", 3), ("A2l", 4), ("A2r", 4), ("A2l", 1), ("E1l", 5), ("E1r", 6), ("E1l", 6), ("A2l", 6), ("Swr", 6), ("Swl", 5), ("A2r", 6),
    ("Swl", 3), ("Swl", 6), ("A2r", 1), ("E1r", 0), ("Swr", 0), ("E1r", 5), ("Swr", 5), ("A2r", 0), ("E0", 6), ("E1l", 0), ("E1l", 2), ("Swl", 0),
    ("R3a", 4), ("A2l", 0), ("R3b", 4), ("A2r", 3), ("Sp", 8), ("Swl", 2), ("A2l", 3), ("E1r", 2), ("E1r", 7), ("E0", 3), ("Swr", 2), ("R3c", 4),
    ("A2l", 2), ("E1r", 8), ("R3a", 6), ("A2r", 5), ("E0", 1), ("A2l", 5), ("E2", 7), ("A2r", 2), ("R4l", 4), ("E1l", 8), ("R4r", 4), ("E0", 0),
    ("R3a", 0), ("Sp", 7), ("Swl", 8), ("R3b", 6), ("R3b", 0), ("A2r", 8), ("R3c", 0), ("E1l", 7), ("E0", 2), ("Swr", 8), ("A2l", 8), ("Swr", 7),
    ("R4l", 6), ("E0", 8), ("R4r", 6), ("E0", 5), ("Swl", 7), ("R3a", 2), ("R5", 4), ("R4l", 0), ("A2l", 7), ("A2r", 7), ("R4r", 0), ("R3b", 2),
    ("R3a", 5), ("E0", 7), ("R3c", 6), ("R3a", 1), ("R3a", 3), ("R3a", 8), ("R5", 6), ("G8r", 4, 0), ("R4r", 2), ("R3c", 2), ("R3b", 3), ("R4l", 2),
    ("R3c", 8), ("R3b", 1), ("R3c", 3), ("R3b", 5), ("R3b", 8), ("R3a", 7), ("G6r", 4), ("G6l", 4), ("R4r", 3), ("R5", 0), ("G8l", 6, 0), ("R4l", 5),
    ("R4r", 8), ("R4r", 5), ("G8r", 6, 0), ("R4l", 8), ("G8l", 4, 0), ("R3c", 7), ("R3b", 7), ("R4l", 1), ("R4r", 1), ("R4l", 3), ("R5", 2),
    ("G8r", 4, -1), ("R4l", 7), ("G6l", 6), ("R4r", 7), ("G8l", 4, -1), ("G7", 4), ("G6r", 6), ("G8r", 0, 0), ("R5", 8), ("R5", 3), ("G6l", 0),
    ("G6r", 0), ("G8l", 6, 1), ("R3c", 1), ("R5", 1), ("R3c", 5), ("G8r", 6, 1), ("R5", 7), ("R5", 5), ("N0", 0), ("G6r", 2), ("G8l", 8, 0),
    ("G6r", 8), ("G6l", 3), ("G8r", 4, 2), ("G6l", 2), ("G6l", 8), ("G6r", 1), ("G7", 0), ("G8r", 8, 0), ("G8l", 7, 0), ("G6l", 1), ("G6r", 3),
    ("G8r", 0, 1), ("G6l", 7), ("N1", 0), ("G6r", 7), ("G6r", 5), ("G6l", 5), ("G8l", 2, 0), ("G7", 6), ("G8r", 7, 0), ("G8l", 6, -1), ("G8r", 2, 0),
    ("G8r", 2, 1), ("G8l", 0, -1), ("G8l", 4, 1), ("G8l", 8, 1), ("G7", 2), ("G7", 8), ("G8l", 0, 2), ("G8r", 8, -1), ("G7", 1), ("G7", 3),
    ("G8l", 1, -1), ("G8r", 0, -1), ("G8r", 2, -1), ("G8r", 0, 2), ("G8l", 0, 1), ("G8r", 7, 1), ("G8l", 2, -1), ("G8r", 3, -1), ("G7", 5),
    ("G8r", 1, 0), ("G8l", 3, 0), ("G8l", 1, 1), ("G8r", 3, 1), ("G7", 7), ("G8r", 8, 1), ("G8r", 4, 1), ("G8l", 3, 1), ("G8r", 3, 0), ("G8l", 4, 2),
    ("G8l", 2, 1), ("G8r", 1, 1), ("G8l", 1, 0), ("N2", 0), ("G8l", 3, -1), ("G8l", 7, -1), ("G8r", 1, -1), ("G8l", 0, 0), ("G8r", 6, -1),
    ("G8r", 6, 2), ("G8l", 8, -1), ("G8l", 1, 2), ("G8l", 5, 1), ("G8r", 1, 2), ("G8r", 7, -1), ("G8r", 5, -1), ("G8r", 5, 0), ("G8l", 5, 0),
    ("G8l", 6, 2), ("G8l", 3, 2), ("G8l", 2, 2), ("G8r", 3, 2), ("G8l", 8, 2), ("G8r", 2, 2), ("G8l", 5, -1), ("G8r", 5, 1), ("G8r", 8, 2),
    ("G8l", 5, 2), ("G8r", 5, 2), ("G8l", 7, 1), ("G8r", 7, 2), ("G8l", 7, 2), ("N3", 0), ("G9", 0), ("G9", 1), ("G9", 4), ("G9", 6), ("G9", 8),
    ("G9", 2), ("G9", 3), ("G9", 7), ("G9", 5),
)


def kernel(
    base_hbm, local_hbm, momentum_hbm, params_ref, new_momentum_ref, rms_ref,
    base_ref, local_ref, momentum_ref, coded_ref,
    full_l, full_r, half_l, half_r, last_l, last_r, part_l, part_r,
    squares_ref, norm_ref, early_ref, load_sem, send_sem, recv_sem,
):
    rows, columns = base_ref.shape
    half = rows // 2
    piece = columns // (SIDE * SIDE)
    replica = lax.axis_index("replica")
    fsdp = lax.axis_index("fsdp")
    at = {"x": replica // SIDE, "z": replica % SIDE}
    near, z_lo = fsdp % 2, fsdp // 8
    y = (fsdp // 2) % 4

    def shifted(axis, step):
        return (at[axis] + step + SIDE) % SIDE

    def device(axis, step):
        x, z = at["x"], at["z"]
        if axis == "x":
            x = shifted("x", step)
        else:
            z = shifted("z", step)
        return (x * SIDE + z, fsdp)

    def fsdp_device(axis, step):
        if axis == "y":
            return (replica, z_lo * 8 + (y + step) % 4 * 2 + near)
        other = (z_lo * 2 + near + step) % 4
        return (replica, other // 2 * 8 + y * 2 + other % 2)

    barrier = pltpu.get_barrier_semaphore()
    peers = [device(axis, step) for axis in ("x", "z") for step in (1, 2, 3)]
    peers += [fsdp_device(axis, step) for axis in ("y", "other") for step in (1, 2, 3)]
    for peer in peers:
        pl.semaphore_signal(barrier, inc=1, device_id=peer, device_id_type=MESH)

    for c, (start, count, first) in enumerate(CHUNKS[:EARLY]):
        for s in range(SIDE):
            x, z = (shifted("x", 2), s) if first == "x" else (s, shifted("z", 2))
            cols = pl.ds(pl.multiple_of((x * SIDE + z) * piece + start * LANES, LANES), count * LANES)
            for i, src in enumerate((base_hbm.at[:, cols], local_hbm.at[0, :, cols])):
                dst = early_ref.at[c, i, s, :, pl.ds(0, count * LANES)]
                pltpu.make_async_copy(src, dst, load_sem.at[9 + c]).start()

    group = SIDE * piece
    loads = {}
    for i, step in enumerate((2, 1, -1, 0)):
        cols = pl.ds(pl.multiple_of(shifted("x", step) * group, LANES), group)
        loads[step] = (
            pltpu.make_async_copy(base_hbm.at[:, cols], base_ref.at[:, cols], load_sem.at[2 * i]),
            pltpu.make_async_copy(local_hbm.at[0, :, cols], local_ref.at[:, cols], load_sem.at[2 * i + 1]),
        )
        for copy in loads[step]:
            copy.start()
    momentum_load = pltpu.make_async_copy(momentum_hbm, momentum_ref, load_sem.at[8])
    momentum_load.start()
    entered = []
    waited = set()
    squares_ref[...] = jnp.zeros_like(squares_ref)

    def loaded(step):
        if step not in waited:
            waited.add(step)
            for copy in loads[step]:
                copy.wait()

    groups = {}

    def send(key, src, dst, target):
        if not entered:
            entered.append(True)
            pl.semaphore_wait(barrier, len(peers))
        together = key
        if key[0] in GROUP:
            together = (GROUP[key[0]], key[-1])
        elif key[0] in ("G_r", "G_l"):
            together = ("G", *key[1:])
        i = groups.setdefault(together, len(groups))
        pltpu.make_async_remote_copy(
            src_ref=src, dst_ref=dst, send_sem=send_sem.at[key[-1]], recv_sem=recv_sem.at[i],
            device_id=target, device_id_type=MESH,
        ).start()

    def wait(sem, sized):
        pltpu.make_async_copy(sized, sized, sem).wait()

    def recv(key, sized):
        if key not in waited:
            waited.add(key)
            wait(recv_sem.at[groups[key]], sized)

    def pieces(count, x, z):
        return coded_ref.at[pl.ds(0, count), pl.ds(0, x), pl.ds(0, z)]

    low, high, every = pl.ds(0, half), pl.ds(half, half), pl.ds(0, rows)

    def column(x, z, block):
        return pl.multiple_of((x * SIDE + z) * piece + block * LANES, LANES)

    def code_block(block, x, z):
        cols = pl.ds(column(x, z, block), LANES)
        code_values(block, x, z, base_ref[:, cols], local_ref[:, cols])

    def code_values(block, x, z, base, local):
        delta = base.astype(jnp.float32) - local.astype(jnp.float32)
        largest = jnp.max(jnp.abs(delta), axis=1, keepdims=True)
        scale = ((largest + 1e-06) * (1.0 / 448.0)).astype(jnp.bfloat16).astype(jnp.float32)
        coded = (delta / scale).astype(jnp.bfloat16).astype(jnp.float32)
        coded_ref[block, x, z] = (coded * scale).astype(jnp.bfloat16)

    def over(start, count, body, unroll=2):
        def step(i, carry):
            body(start + i // SIDE, i % SIDE)
            return carry
        lax.fori_loop(0, count * SIDE, step, 0, unroll=unroll)

    def blocks(start, count, body):
        def step(i, carry):
            body(start + i)
            return carry
        lax.fori_loop(0, count, step, 0)

    def f32(value):
        return value.astype(jnp.float32)

    steps = {}
    for c, (start, count, first) in enumerate(CHUNKS):
        second = "z" if first == "x" else "x"
        ks = pl.ds(start, count)

        def xz(f, s, first=first):
            return (f, s) if first == "x" else (s, f)

        def row_of(f, rs, ks=ks, first=first):
            if first == "x":
                return coded_ref.at[ks, f, :, rs]
            return coded_ref.at[ks, :, f, rs]

        def piece_of(f, s, rs, ks=ks, xz=xz):
            return coded_ref.at[(ks, *xz(f, s), rs)]

        def gathered(f, s, rs, start=start, count=count, xz=xz):
            return params_ref.at[rs, pl.ds(column(*xz(f, s), start), count * LANES)]

        def code(f_step, start=start, count=count, first=first, xz=xz):
            if first == "x":
                loaded(f_step)
            else:
                for step in (2, 1, -1, 0):
                    loaded(step)
            f = shifted(first, f_step)
            over(start, count, lambda block, s: code_block(block, *xz(f, s)))


        def E2(c=c, start=start, count=count, first=first, code=code, xz=xz):
            if c >= EARLY:
                code(2)
                return
            wait(load_sem.at[9 + c], early_ref.at[c, :, :, :, pl.ds(0, count * LANES)])
            f = shifted(first, 2)

            def early(block, s):
                cols = pl.ds(pl.multiple_of((block - start) * LANES, LANES), LANES)
                code_values(block, *xz(f, s), early_ref[c, 0, s, :, cols], early_ref[c, 1, s, :, cols])
            over(start, count, early)

        def E1r(code=code):
            code(1)

        def E1l(code=code):
            code(-1)

        def E0(code=code):
            code(0)

        def Sp(c=c, ks=ks, first=first, row_of=row_of):
            far = shifted(first, 2)
            send(("p_r", c), row_of(far, low), half_l.at[ks], device(first, 1))
            send(("p_l", c), row_of(far, high), half_r.at[ks], device(first, -1))

        def Swr(c=c, ks=ks, first=first, row_of=row_of):
            send(("w_r", c), row_of(shifted(first, 1), high), full_l.at[ks, :, high], device(first, 1))

        def Swl(c=c, ks=ks, first=first, row_of=row_of):
            send(("w_l", c), row_of(shifted(first, -1), low), full_r.at[ks, :, low], device(first, -1))

        def join(name, step, rs, got, into, c=c, ks=ks, start=start, count=count, first=first, row_of=row_of, xz=xz):
            f = shifted(first, step)
            recv(("p", c), pieces(count, 4, 1))

            def add(block, s):
                index = (block, *xz(f, s), rs)
                coded_ref[index] = (f32(coded_ref[index]) + f32(got[block, s])).astype(jnp.bfloat16)
            over(start, count, add)
            send(("s_" + name, c), row_of(f, rs), into.at[ks, :, rs], device(first, step))

        def A2r(join=join):
            join("r", 1, low, half_l, full_l)

        def A2l(join=join):
            join("l", -1, high, half_r, full_r)

        def total_at(s, start=start, count=count, first=first, xz=xz):
            def add(block):
                index = (block, *xz(at[first], s))
                total = f32(coded_ref[index]) + f32(full_l[block, s]) + f32(full_r[block, s])
                coded_ref[index] = total.astype(jnp.bfloat16)
            blocks(start, count, add)

        def R3a(c=c, ks=ks, count=count, first=first, second=second, piece_of=piece_of, total_at=total_at):
            recv(("first", c), pieces(count, 4, 2))
            far = shifted(second, 2)
            total_at(far)
            send(("P_r", c), piece_of(at[first], far, low), part_l.at[ks], device(second, 1))
            send(("P_l", c), piece_of(at[first], far, high), part_r.at[ks], device(second, -1))

        def R3b(c=c, ks=ks, first=first, second=second, piece_of=piece_of, total_at=total_at):
            for name, step, rs, into in (("r", 1, high, last_l), ("l", -1, low, last_r)):
                s = shifted(second, step)
                total_at(s)
                send(("W_" + name, c), piece_of(at[first], s, rs), into.at[ks, rs], device(second, step))

        def R3c(second=second, total_at=total_at):
            total_at(at[second])

        def last_join(name, step, rs, got, into, c=c, ks=ks, start=start, count=count, first=first, second=second,
                      piece_of=piece_of, xz=xz):
            s = shifted(second, step)
            recv(("P", c), pieces(count, 1, 1))

            def add(block):
                index = (block, *xz(at[first], s), rs)
                coded_ref[index] = (f32(coded_ref[index]) + f32(got[block])).astype(jnp.bfloat16)
            blocks(start, count, add)
            send(("S_" + name, c), piece_of(at[first], s, rs), into.at[ks, rs], device(second, step))

        def R4r(last_join=last_join):
            last_join("r", 1, low, part_l, last_l)

        def R4l(last_join=last_join):
            last_join("l", -1, high, part_r, last_r)

        def spread(s, c=c, first=first, second=second, gathered=gathered):
            for name, step in (("r", 1), ("l", -1)):
                part = gathered(at[first], shifted(second, s), every)
                send(("G_" + name, s, c), part, part, device(first, step))

        def R5(c=c, start=start, count=count, first=first, second=second, gathered=gathered, spread=spread):
            recv(("second", c), pieces(count, 1, 2))
            if "momentum" not in waited:
                waited.add("momentum")
                momentum_load.wait()

            def update(block):
                x, z = at["x"], at["z"]
                total = f32(coded_ref[block, x, z]) + f32(last_l[block]) + f32(last_r[block])
                grad = total * (1.0 / (SIDE * SIDE))
                squares_ref[...] += jnp.sum((grad * grad).reshape(rows // 8, 8, LANES), axis=0)
                own = pl.ds(pl.multiple_of(block * LANES, LANES), LANES)
                new_momentum = momentum_decay * momentum_ref[:, own] + grad
                new_momentum_ref[:, own] = new_momentum
                cols = pl.ds(column(x, z, block), LANES)
                stepped = f32(base_ref[:, cols]) - outer_rate * (momentum_decay * new_momentum + grad)
                params_ref[:, cols] = stepped.astype(jnp.bfloat16)
            blocks(start, count, update)
            mine = gathered(at[first], at[second], every)
            send(("g_r", c), mine, mine, device(second, 1))
            send(("g_l", c), mine, mine, device(second, -1))
            spread(0)

        def pass_on(name, step, rs, c=c, count=count, first=first, second=second, gathered=gathered, spread=spread):
            recv(("g", c), pieces(count, 1, 2))
            passed = gathered(at[first], shifted(second, -step), rs)
            send(("h_" + name, c), passed, passed, device(second, step))
            spread(-step)

        def G6r(pass_on=pass_on):
            pass_on("r", 1, low)

        def G6l(pass_on=pass_on):
            pass_on("l", -1, high)

        def G7(c=c, count=count, spread=spread):
            recv(("far", c), pieces(count, 1, 1))
            spread(2)

        def last_pass(s, name, step, rs, c=c, count=count, first=first, second=second, gathered=gathered):
            recv(("G", s, c), pieces(count, 1, 2))
            passed = gathered(shifted(first, -step), shifted(second, s), rs)
            send(("H_" + name, s, c), passed, passed, device(first, step))

        def G9(c=c, count=count):
            recv(("last", c), pieces(count, 4, 1))

        for step in (E2, E1r, E1l, E0, Sp, Swr, Swl, A2r, A2l, R3a, R3b, R3c, R4r, R4l, R5, G6r, G6l, G7, G9):
            steps[step.__name__, c] = step
        for s in (0, 1, -1, 2):
            steps["G8r", c, s] = functools.partial(last_pass, s, "r", 1, low)
            steps["G8l", c, s] = functools.partial(last_pass, s, "l", -1, high)

    def norm_round(i, place, target):
        for step in (1, 2, 3):
            send((f"n{i}", len(CHUNKS)), norm_ref.at[i, place], norm_ref.at[i, place], target(step))

    def norm_sum(i):
        recv((f"n{i}", len(CHUNKS)), norm_ref.at[0, pl.ds(0, 3)])
        return norm_ref[i, 0] + norm_ref[i, 1] + norm_ref[i, 2] + norm_ref[i, 3]

    other = z_lo * 2 + near

    def N0():
        norm_ref[0, at["x"]] = squares_ref[...]
        norm_round(0, at["x"], lambda step: device("x", step))

    def N1():
        norm_ref[1, at["z"]] = norm_sum(0)
        norm_round(1, at["z"], lambda step: device("z", step))

    def N2():
        norm_ref[2, y] = norm_sum(1)
        norm_round(2, y, lambda step: fsdp_device("y", step))

    def N3():
        norm_ref[3, other] = norm_sum(2)
        norm_round(3, other, lambda step: fsdp_device("other", step))

    for step in (N0, N1, N2, N3):
        steps[step.__name__, 0] = step

    for key in ORDER:
        steps[key]()
    total = jnp.sum(norm_sum(3), axis=(0, 1), keepdims=True)
    entries = rows * columns * 16
    rms_ref[...] = jnp.broadcast_to(jnp.sqrt(total / entries), rms_ref.shape)
    for c, (_, count, _) in enumerate(CHUNKS):
        wide, high_, deep = SENT[count]
        wait(send_sem.at[c], coded_ref.at[pl.ds(0, wide), pl.ds(0, high_), pl.ds(0, deep)])
    wait(send_sem.at[len(CHUNKS)], norm_ref.at[pl.ds(0, 3)])


second_of = {"x": "z", "z": "x"}
SPLIT = 1
EARLY = 2
RECEIVES = len(CHUNKS) * 11 + 4
GROUP = {
    "p_r": "p", "p_l": "p", "P_r": "P", "P_l": "P", "g_r": "g", "g_l": "g",
    "w_r": "first", "w_l": "first", "s_r": "first", "s_l": "first",
    "W_r": "second", "W_l": "second", "S_r": "second", "S_l": "second",
    "h_r": "far", "h_l": "far", "H_r": "last", "H_l": "last",
}
SENT = {1: (10, 3, 1), 2: (5, 4, 3), 3: (10, 3, 3), 4: (10, 4, 3)}


def write_out(params_ref, momentum_ref, rms_ref, params_hbm, momentum_hbm, rms_hbm, sem):
    copies = [pltpu.make_async_copy(rms_ref, rms_hbm, sem.at[0])]
    for src, dst in ((params_ref, params_hbm), (momentum_ref, momentum_hbm)):
        step = src.shape[0] // SPLIT
        for i in range(SPLIT):
            part = pl.ds(i * step, step)
            copies.append(pltpu.make_async_copy(src.at[part], dst.at[part], sem.at[len(copies)]))
    for copy in copies:
        copy.start()
    for copy in copies:
        copy.wait()


def per_device(base, local, momentum):
    rows, columns = base.shape
    piece = columns // (SIDE * SIDE)
    number = piece // LANES
    half = rows // 2
    bf16 = functools.partial(pltpu.VMEM, dtype=jnp.bfloat16)
    vmem = pl.BlockSpec(memory_space=pltpu.VMEM)
    new_params, new_momentum, rms = pl.pallas_call(
        kernel,
        out_shape=(
            pltpu.VMEM((rows, columns), jnp.bfloat16),
            pltpu.VMEM((rows, piece), jnp.float32),
            pltpu.VMEM((1, 1), jnp.float32),
        ),
        in_specs=[pl.BlockSpec(memory_space=pltpu.HBM)] * 3,
        out_specs=(vmem, vmem, vmem),
        scratch_shapes=[
            bf16((rows, columns)),
            bf16((rows, columns)),
            pltpu.VMEM((rows, piece), jnp.float32),
            bf16((number, SIDE, SIDE, rows, LANES)),
            bf16((number, SIDE, rows, LANES)),
            bf16((number, SIDE, rows, LANES)),
            bf16((number, SIDE, half, LANES)),
            bf16((number, SIDE, half, LANES)),
            bf16((number, rows, LANES)),
            bf16((number, rows, LANES)),
            bf16((number, half, LANES)),
            bf16((number, half, LANES)),
            pltpu.VMEM((8, LANES), jnp.float32),
            pltpu.VMEM((4, 4, 8, LANES), jnp.float32),
            bf16((EARLY, 2, SIDE, rows, max(c[1] for c in CHUNKS[:EARLY]) * LANES)),
            pltpu.SemaphoreType.DMA((9 + EARLY,)),
            pltpu.SemaphoreType.DMA((len(CHUNKS) + 1,)),
            pltpu.SemaphoreType.DMA((RECEIVES,)),
        ],
        compiler_params=pltpu.CompilerParams(
            collective_id=0, has_side_effects=True, vmem_limit_bytes=24 * 2**20
        ),
        name="outer_step",
    )(*(pltpu.with_memory_space_constraint(a, pltpu.HBM) for a in (base, local, momentum)))
    hbm = pl.BlockSpec(memory_space=pltpu.HBM)
    new_params, new_momentum, rms = pl.pallas_call(
        write_out,
        out_shape=(
            pltpu.HBM((rows, columns), jnp.bfloat16),
            pltpu.HBM((rows, piece), jnp.float32),
            pltpu.HBM((1, 1), jnp.float32),
        ),
        in_specs=[vmem] * 3,
        out_specs=(hbm,) * 3,
        scratch_shapes=[pltpu.SemaphoreType.DMA((2 * SPLIT + 1,))],
        compiler_params=pltpu.CompilerParams(vmem_limit_bytes=2**20),
        name="write_out",
    )(*(pltpu.with_memory_space_constraint(a, pltpu.VMEM) for a in (new_params, new_momentum, rms)))
    return (new_params, new_momentum, rms[0, 0])


def solution(mesh):
    return jax.shard_map(
        per_device,
        mesh=mesh,
        in_specs=(P("fsdp", None), P("replica", "fsdp", None), P("fsdp", "replica")),
        out_specs=(P("fsdp", None), P("fsdp", "replica"), P()),
        check_vma=False,
    )
```

```python
import functools

import jax
import jax.numpy as jnp
from jax import lax
from jax.experimental import pallas as pl
from jax.experimental.pallas import tpu as pltpu
from jax.sharding import PartitionSpec as P

MESH = pl.DeviceIdType.MESH
LANES = 128
SIDE = 4
outer_rate = 0.7
momentum_decay = 0.9

CHUNKS = (
    (0, 2, "x"),
    (11, 1, "z"),
    (2, 2, "x"),
    (12, 1, "z"),
    (4, 2, "x"),
    (13, 1, "z"),
    (6, 2, "x"),
    (8, 2, "x"),
    (10, 1, "x"),
)
ORDER = (
    ("E2", 0), ("Sp", 0), ("E2", 1), ("E2", 6), ("E2", 4), ("Sp", 1), ("Sp", 4), ("Sp", 6), ("E1l", 4), ("E1r", 4), ("E2", 5), ("Swl", 4), ("Swr", 4),
    ("Sp", 5), ("E2", 3), ("E2", 2), ("E1r", 3), ("E2", 8), ("Sp", 2), ("Sp", 3), ("E1l", 1), ("E1r", 1), ("Swl", 1), ("Swr", 3), ("E0", 4),
    ("Swr", 1), ("E1l", 3), ("A2l", 4), ("A2r", 4), ("A2l", 1), ("E1l", 5), ("E1r", 6), ("E1l", 6), ("A2l", 6), ("Swr", 6), ("Swl", 5), ("A2r", 6),
    ("Swl", 3), ("Swl", 6), ("A2r", 1), ("E1r", 0), ("Swr", 0), ("E1r", 5), ("Swr", 5), ("A2r", 0), ("E0", 6), ("E1l", 0), ("E1l", 2), ("Swl", 0),
    ("R3a", 4), ("A2l", 0), ("R3b", 4), ("A2r", 3), ("Sp", 8), ("Swl", 2), ("A2l", 3), ("E1r", 2), ("E1r", 7), ("E0", 3), ("Swr", 2), ("R3c", 4),
    ("A2l", 2), ("E1r", 8), ("R3a", 6), ("A2r", 5), ("E0", 1), ("A2l", 5), ("E2", 7), ("A2r", 2), ("R4l", 4), ("E1l", 8), ("R4r", 4), ("E0", 0),
    ("R3a", 0), ("Sp", 7), ("Swl", 8), ("R3b", 6), ("R3b", 0), ("A2r", 8), ("R3c", 0), ("E1l", 7), ("E0", 2), ("Swr", 8), ("A2l", 8), ("Swr", 7),
    ("R4l", 6), ("E0", 8), ("R4r", 6), ("E0", 5), ("Swl", 7), ("R3a", 2), ("R5", 4), ("R4l", 0), ("A2l", 7), ("A2r", 7), ("R4r", 0), ("R3b", 2),
    ("R3a", 5), ("E0", 7), ("R3c", 6), ("R3a", 1), ("R3a", 3), ("R3a", 8), ("R5", 6), ("G8r", 4, 0), ("R4r", 2), ("R3c", 2), ("R3b", 3), ("R4l", 2),
    ("R3c", 8), ("R3b", 1), ("R3c", 3), ("R3b", 5), ("R3b", 8), ("R3a", 7), ("G6r", 4), ("G6l", 4), ("R4r", 3), ("R5", 0), ("G8l", 6, 0), ("R4l", 5),
    ("R4r", 8), ("R4r", 5), ("G8r", 6, 0), ("R4l", 8), ("G8l", 4, 0), ("R3c", 7), ("R3b", 7), ("R4l", 1), ("R4r", 1), ("R4l", 3), ("R5", 2),
    ("G8r", 4, -1), ("R4l", 7), ("G6l", 6), ("R4r", 7), ("G8l", 4, -1), ("G7", 4), ("G6r", 6), ("G8r", 0, 0), ("R5", 8), ("R5", 3), ("G6l", 0),
    ("G6r", 0), ("G8l", 6, 1), ("R3c", 1), ("R5", 1), ("R3c", 5), ("G8r", 6, 1), ("R5", 7), ("R5", 5), ("N0", 0), ("G6r", 2), ("G8l", 8, 0),
    ("G6r", 8), ("G6l", 3), ("G8r", 4, 2), ("G6l", 2), ("G6l", 8), ("G6r", 1), ("G7", 0), ("G8r", 8, 0), ("G8l", 7, 0), ("G6l", 1), ("G6r", 3),
    ("G8r", 0, 1), ("G6l", 7), ("N1", 0), ("G6r", 7), ("G6r", 5), ("G6l", 5), ("G8l", 2, 0), ("G7", 6), ("G8r", 7, 0), ("G8l", 6, -1), ("G8r", 2, 0),
    ("G8r", 2, 1), ("G8l", 0, -1), ("G8l", 4, 1), ("G8l", 8, 1), ("G7", 2), ("G7", 8), ("G8l", 0, 2), ("G8r", 8, -1), ("G7", 1), ("G7", 3),
    ("G8l", 1, -1), ("G8r", 0, -1), ("G8r", 2, -1), ("G8r", 0, 2), ("G8l", 0, 1), ("G8r", 7, 1), ("G8l", 2, -1), ("G8r", 3, -1), ("G7", 5),
    ("G8r", 1, 0), ("G8l", 3, 0), ("G8l", 1, 1), ("G8r", 3, 1), ("G7", 7), ("G8r", 8, 1), ("G8r", 4, 1), ("G8l", 3, 1), ("G8r", 3, 0), ("G8l", 4, 2),
    ("G8l", 2, 1), ("G8r", 1, 1), ("G8l", 1, 0), ("N2", 0), ("G8l", 3, -1), ("G8l", 7, -1), ("G8r", 1, -1), ("G8l", 0, 0), ("G8r", 6, -1),
    ("G8r", 6, 2), ("G8l", 8, -1), ("G8l", 1, 2), ("G8l", 5, 1), ("G8r", 1, 2), ("G8r", 7, -1), ("G8r", 5, -1), ("G8r", 5, 0), ("G8l", 5, 0),
    ("G8l", 6, 2), ("G8l", 3, 2), ("G8l", 2, 2), ("G8r", 3, 2), ("G8l", 8, 2), ("G8r", 2, 2), ("G8l", 5, -1), ("G8r", 5, 1), ("G8r", 8, 2),
    ("G8l", 5, 2), ("G8r", 5, 2), ("G8l", 7, 1), ("G8r", 7, 2), ("G8l", 7, 2), ("N3", 0), ("G9", 0), ("G9", 1), ("G9", 4), ("G9", 6), ("G9", 8),
    ("G9", 2), ("G9", 3), ("G9", 7), ("G9", 5),
)


def kernel(
    base_hbm, local_hbm, momentum_hbm, params_ref, new_momentum_ref, rms_ref,
    base_ref, local_ref, momentum_ref, coded_ref,
    full_l, full_r, half_l, half_r, last_l, last_r, part_l, part_r,
    squares_ref, norm_ref, early_ref, load_sem, send_sem, recv_sem,
):
    rows, columns = base_ref.shape
    half = rows // 2
    piece = columns // (SIDE * SIDE)
    replica = lax.axis_index("replica")
    fsdp = lax.axis_index("fsdp")
    at = {"x": replica // SIDE, "z": replica % SIDE}
    near, z_lo = fsdp % 2, fsdp // 8
    y = (fsdp // 2) % 4

    def shifted(axis, step):
        return (at[axis] + step + SIDE) % SIDE

    def device(axis, step):
        x, z = at["x"], at["z"]
        if axis == "x":
            x = shifted("x", step)
        else:
            z = shifted("z", step)
        return (x * SIDE + z, fsdp)

    def fsdp_device(axis, step):
        if axis == "y":
            return (replica, z_lo * 8 + (y + step) % 4 * 2 + near)
        other = (z_lo * 2 + near + step) % 4
        return (replica, other // 2 * 8 + y * 2 + other % 2)

    barrier = pltpu.get_barrier_semaphore()
    peers = [device(axis, step) for axis in ("x", "z") for step in (1, 2, 3)]
    peers += [fsdp_device(axis, step) for axis in ("y", "other") for step in (1, 2, 3)]
    for peer in peers:
        pl.semaphore_signal(barrier, inc=1, device_id=peer, device_id_type=MESH)

    for c, (start, count, first) in enumerate(CHUNKS[:EARLY]):
        for s in range(SIDE):
            x, z = (shifted("x", 2), s) if first == "x" else (s, shifted("z", 2))
            cols = pl.ds(pl.multiple_of((x * SIDE + z) * piece + start * LANES, LANES), count * LANES)
            for i, src in enumerate((base_hbm.at[:, cols], local_hbm.at[0, :, cols])):
                dst = early_ref.at[c, i, s, :, pl.ds(0, count * LANES)]
                pltpu.make_async_copy(src, dst, load_sem.at[9 + c]).start()

    group = SIDE * piece
    loads = {}
    for i, step in enumerate((2, 1, -1, 0)):
        cols = pl.ds(pl.multiple_of(shifted("x", step) * group, LANES), group)
        loads[step] = (
            pltpu.make_async_copy(base_hbm.at[:, cols], base_ref.at[:, cols], load_sem.at[2 * i]),
            pltpu.make_async_copy(local_hbm.at[0, :, cols], local_ref.at[:, cols], load_sem.at[2 * i + 1]),
        )
        for copy in loads[step]:
            copy.start()
    momentum_load = pltpu.make_async_copy(momentum_hbm, momentum_ref, load_sem.at[8])
    momentum_load.start()
    entered = []
    waited = set()
    squares_ref[...] = jnp.zeros_like(squares_ref)

    def loaded(step):
        if step not in waited:
            waited.add(step)
            for copy in loads[step]:
                copy.wait()

    groups = {}

    def slot(key):
        if key[:2] == ("G", 0):
            return ("p", key[-1])
        return (REUSED.get(key[0], key[0]), *key[1:])

    def send(key, src, dst, target):
        if not entered:
            entered.append(True)
            pl.semaphore_wait(barrier, len(peers))
        together = key
        if key[0] in GROUP:
            together = (GROUP[key[0]], key[-1])
        elif key[0] in ("G_r", "G_l"):
            together = ("G", *key[1:])
        i = groups.setdefault(slot(together), len(groups))
        pltpu.make_async_remote_copy(
            src_ref=src, dst_ref=dst, send_sem=send_sem.at[key[-1]], recv_sem=recv_sem.at[i],
            device_id=target, device_id_type=MESH,
        ).start()

    def wait(sem, sized):
        pltpu.make_async_copy(sized, sized, sem).wait()

    def recv(key, sized):
        if key not in waited:
            waited.add(key)
            wait(recv_sem.at[groups[slot(key)]], sized)

    def pieces(count, x, z):
        return coded_ref.at[pl.ds(0, count), pl.ds(0, x), pl.ds(0, z)]

    low, high, every = pl.ds(0, half), pl.ds(half, half), pl.ds(0, rows)

    def column(x, z, block):
        return pl.multiple_of((x * SIDE + z) * piece + block * LANES, LANES)

    def code_block(block, x, z):
        cols = pl.ds(column(x, z, block), LANES)
        code_values(block, x, z, base_ref[:, cols], local_ref[:, cols])

    def code_values(block, x, z, base, local):
        delta = base.astype(jnp.float32) - local.astype(jnp.float32)
        largest = jnp.max(jnp.abs(delta), axis=1, keepdims=True)
        scale = ((largest + 1e-06) * (1.0 / 448.0)).astype(jnp.bfloat16).astype(jnp.float32)
        coded = (delta / scale).astype(jnp.bfloat16).astype(jnp.float32)
        coded_ref[block, x, z] = (coded * scale).astype(jnp.bfloat16)

    def over(start, count, body, unroll=2):
        def step(i, carry):
            body(start + i // SIDE, i % SIDE)
            return carry
        lax.fori_loop(0, count * SIDE, step, 0, unroll=unroll)

    def blocks(start, count, body):
        def step(i, carry):
            body(start + i)
            return carry
        lax.fori_loop(0, count, step, 0)

    def f32(value):
        return value.astype(jnp.float32)

    steps = {}
    for c, (start, count, first) in enumerate(CHUNKS):
        second = "z" if first == "x" else "x"
        ks = pl.ds(start, count)

        def xz(f, s, first=first):
            return (f, s) if first == "x" else (s, f)

        def row_of(f, rs, ks=ks, first=first):
            if first == "x":
                return coded_ref.at[ks, f, :, rs]
            return coded_ref.at[ks, :, f, rs]

        def piece_of(f, s, rs, ks=ks, xz=xz):
            return coded_ref.at[(ks, *xz(f, s), rs)]

        def gathered(f, s, rs, start=start, count=count, xz=xz):
            return params_ref.at[rs, pl.ds(column(*xz(f, s), start), count * LANES)]

        def code(f_step, start=start, count=count, first=first, xz=xz):
            if first == "x":
                loaded(f_step)
            else:
                for step in (2, 1, -1, 0):
                    loaded(step)
            f = shifted(first, f_step)
            over(start, count, lambda block, s: code_block(block, *xz(f, s)))


        def E2(c=c, start=start, count=count, first=first, code=code, xz=xz):
            if c >= EARLY:
                code(2)
                return
            wait(load_sem.at[9 + c], early_ref.at[c, :, :, :, pl.ds(0, count * LANES)])
            f = shifted(first, 2)

            def early(block, s):
                cols = pl.ds(pl.multiple_of((block - start) * LANES, LANES), LANES)
                code_values(block, *xz(f, s), early_ref[c, 0, s, :, cols], early_ref[c, 1, s, :, cols])
            over(start, count, early)

        def E1r(code=code):
            code(1)

        def E1l(code=code):
            code(-1)

        def E0(code=code):
            code(0)

        def Sp(c=c, ks=ks, first=first, row_of=row_of):
            far = shifted(first, 2)
            send(("p_r", c), row_of(far, low), half_l.at[ks], device(first, 1))
            send(("p_l", c), row_of(far, high), half_r.at[ks], device(first, -1))

        def Swr(c=c, ks=ks, first=first, row_of=row_of):
            send(("w_r", c), row_of(shifted(first, 1), high), full_l.at[ks, :, high], device(first, 1))

        def Swl(c=c, ks=ks, first=first, row_of=row_of):
            send(("w_l", c), row_of(shifted(first, -1), low), full_r.at[ks, :, low], device(first, -1))

        def join(name, step, rs, got, into, c=c, ks=ks, start=start, count=count, first=first, row_of=row_of, xz=xz):
            f = shifted(first, step)
            recv(("p", c), pieces(count, 4, 1))

            def add(block, s):
                index = (block, *xz(f, s), rs)
                coded_ref[index] = (f32(coded_ref[index]) + f32(got[block, s])).astype(jnp.bfloat16)
            over(start, count, add)
            send(("s_" + name, c), row_of(f, rs), into.at[ks, :, rs], device(first, step))

        def A2r(join=join):
            join("r", 1, low, half_l, full_l)

        def A2l(join=join):
            join("l", -1, high, half_r, full_r)

        def total_at(s, start=start, count=count, first=first, xz=xz):
            def add(block):
                index = (block, *xz(at[first], s))
                total = f32(coded_ref[index]) + f32(full_l[block, s]) + f32(full_r[block, s])
                coded_ref[index] = total.astype(jnp.bfloat16)
            blocks(start, count, add)

        def R3a(c=c, ks=ks, count=count, first=first, second=second, piece_of=piece_of, total_at=total_at):
            recv(("first", c), pieces(count, 4, 2))
            far = shifted(second, 2)
            total_at(far)
            send(("P_r", c), piece_of(at[first], far, low), part_l.at[ks], device(second, 1))
            send(("P_l", c), piece_of(at[first], far, high), part_r.at[ks], device(second, -1))

        def R3b(c=c, ks=ks, first=first, second=second, piece_of=piece_of, total_at=total_at):
            for name, step, rs, into in (("r", 1, high, last_l), ("l", -1, low, last_r)):
                s = shifted(second, step)
                total_at(s)
                send(("W_" + name, c), piece_of(at[first], s, rs), into.at[ks, rs], device(second, step))

        def R3c(second=second, total_at=total_at):
            total_at(at[second])

        def last_join(name, step, rs, got, into, c=c, ks=ks, start=start, count=count, first=first, second=second,
                      piece_of=piece_of, xz=xz):
            s = shifted(second, step)
            recv(("P", c), pieces(count, 1, 1))

            def add(block):
                index = (block, *xz(at[first], s), rs)
                coded_ref[index] = (f32(coded_ref[index]) + f32(got[block])).astype(jnp.bfloat16)
            blocks(start, count, add)
            send(("S_" + name, c), piece_of(at[first], s, rs), into.at[ks, rs], device(second, step))

        def R4r(last_join=last_join):
            last_join("r", 1, low, part_l, last_l)

        def R4l(last_join=last_join):
            last_join("l", -1, high, part_r, last_r)

        def spread(s, c=c, first=first, second=second, gathered=gathered):
            for name, step in (("r", 1), ("l", -1)):
                part = gathered(at[first], shifted(second, s), every)
                send(("G_" + name, s, c), part, part, device(first, step))

        def R5(c=c, start=start, count=count, first=first, second=second, gathered=gathered, spread=spread):
            recv(("second", c), pieces(count, 1, 2))
            if "momentum" not in waited:
                waited.add("momentum")
                momentum_load.wait()

            def update(block):
                x, z = at["x"], at["z"]
                total = f32(coded_ref[block, x, z]) + f32(last_l[block]) + f32(last_r[block])
                grad = total * (1.0 / (SIDE * SIDE))
                squares_ref[...] += jnp.sum((grad * grad).reshape(rows // 8, 8, LANES), axis=0)
                own = pl.ds(pl.multiple_of(block * LANES, LANES), LANES)
                new_momentum = momentum_decay * momentum_ref[:, own] + grad
                new_momentum_ref[:, own] = new_momentum
                cols = pl.ds(column(x, z, block), LANES)
                stepped = f32(base_ref[:, cols]) - outer_rate * (momentum_decay * new_momentum + grad)
                params_ref[:, cols] = stepped.astype(jnp.bfloat16)
            blocks(start, count, update)
            mine = gathered(at[first], at[second], every)
            send(("g_r", c), mine, mine, device(second, 1))
            send(("g_l", c), mine, mine, device(second, -1))
            spread(0)

        def pass_on(name, step, rs, c=c, count=count, first=first, second=second, gathered=gathered, spread=spread):
            recv(("g", c), pieces(count, 1, 2))
            passed = gathered(at[first], shifted(second, -step), rs)
            send(("h_" + name, c), passed, passed, device(second, step))
            spread(-step)

        def G6r(pass_on=pass_on):
            pass_on("r", 1, low)

        def G6l(pass_on=pass_on):
            pass_on("l", -1, high)

        def G7(c=c, count=count, spread=spread):
            recv(("far", c), pieces(count, 1, 1))
            spread(2)

        def last_pass(s, name, step, rs, c=c, count=count, first=first, second=second, gathered=gathered):
            recv(("G", s, c), pieces(count, 1, 2))
            passed = gathered(shifted(first, -step), shifted(second, s), rs)
            send(("H_" + name, s, c), passed, passed, device(first, step))

        def G9(c=c, count=count):
            recv(("last", c), pieces(count, 4, 1))

        for step in (E2, E1r, E1l, E0, Sp, Swr, Swl, A2r, A2l, R3a, R3b, R3c, R4r, R4l, R5, G6r, G6l, G7, G9):
            steps[step.__name__, c] = step
        for s in (0, 1, -1, 2):
            steps["G8r", c, s] = functools.partial(last_pass, s, "r", 1, low)
            steps["G8l", c, s] = functools.partial(last_pass, s, "l", -1, high)

    def norm_round(i, place, target):
        for step in (1, 2, 3):
            send((f"n{i}", len(CHUNKS)), norm_ref.at[i, place], norm_ref.at[i, place], target(step))

    def norm_sum(i):
        recv((f"n{i}", len(CHUNKS)), norm_ref.at[0, pl.ds(0, 3)])
        return norm_ref[i, 0] + norm_ref[i, 1] + norm_ref[i, 2] + norm_ref[i, 3]

    other = z_lo * 2 + near

    def N0():
        norm_ref[0, at["x"]] = squares_ref[...]
        norm_round(0, at["x"], lambda step: device("x", step))

    def N1():
        norm_ref[1, at["z"]] = norm_sum(0)
        norm_round(1, at["z"], lambda step: device("z", step))

    def N2():
        norm_ref[2, y] = norm_sum(1)
        norm_round(2, y, lambda step: fsdp_device("y", step))

    def N3():
        norm_ref[3, other] = norm_sum(2)
        norm_round(3, other, lambda step: fsdp_device("other", step))

    for step in (N0, N1, N2, N3):
        steps[step.__name__, 0] = step

    for key in ORDER:
        steps[key]()
    total = jnp.sum(norm_sum(3), axis=(0, 1), keepdims=True)
    entries = rows * columns * 16
    rms_ref[...] = jnp.broadcast_to(jnp.sqrt(total / entries), rms_ref.shape)
    for c, (_, count, _) in enumerate(CHUNKS):
        wide, high_, deep = SENT[count]
        wait(send_sem.at[c], coded_ref.at[pl.ds(0, wide), pl.ds(0, high_), pl.ds(0, deep)])
    wait(send_sem.at[len(CHUNKS)], norm_ref.at[pl.ds(0, 3)])


second_of = {"x": "z", "z": "x"}
SPLIT = 1
EARLY = 2
RECEIVES = len(CHUNKS) * 7 + 4
REUSED = {"g": "P", "last": "first", "far": "second"}
GROUP = {
    "p_r": "p", "p_l": "p", "P_r": "P", "P_l": "P", "g_r": "g", "g_l": "g",
    "w_r": "first", "w_l": "first", "s_r": "first", "s_l": "first",
    "W_r": "second", "W_l": "second", "S_r": "second", "S_l": "second",
    "h_r": "far", "h_l": "far", "H_r": "last", "H_l": "last",
}
SENT = {1: (10, 3, 1), 2: (5, 4, 3), 3: (10, 3, 3), 4: (10, 4, 3)}


def write_out(params_ref, momentum_ref, rms_ref, params_hbm, momentum_hbm, rms_hbm, sem):
    copies = [pltpu.make_async_copy(rms_ref, rms_hbm, sem.at[0])]
    for src, dst in ((params_ref, params_hbm), (momentum_ref, momentum_hbm)):
        step = src.shape[0] // SPLIT
        for i in range(SPLIT):
            part = pl.ds(i * step, step)
            copies.append(pltpu.make_async_copy(src.at[part], dst.at[part], sem.at[len(copies)]))
    for copy in copies:
        copy.start()
    for copy in copies:
        copy.wait()


def per_device(base, local, momentum):
    rows, columns = base.shape
    piece = columns // (SIDE * SIDE)
    number = piece // LANES
    half = rows // 2
    bf16 = functools.partial(pltpu.VMEM, dtype=jnp.bfloat16)
    vmem = pl.BlockSpec(memory_space=pltpu.VMEM)
    new_params, new_momentum, rms = pl.pallas_call(
        kernel,
        out_shape=(
            pltpu.VMEM((rows, columns), jnp.bfloat16),
            pltpu.VMEM((rows, piece), jnp.float32),
            pltpu.VMEM((1, 1), jnp.float32),
        ),
        in_specs=[pl.BlockSpec(memory_space=pltpu.HBM)] * 3,
        out_specs=(vmem, vmem, vmem),
        scratch_shapes=[
            bf16((rows, columns)),
            bf16((rows, columns)),
            pltpu.VMEM((rows, piece), jnp.float32),
            bf16((number, SIDE, SIDE, rows, LANES)),
            bf16((number, SIDE, rows, LANES)),
            bf16((number, SIDE, rows, LANES)),
            bf16((number, SIDE, half, LANES)),
            bf16((number, SIDE, half, LANES)),
            bf16((number, rows, LANES)),
            bf16((number, rows, LANES)),
            bf16((number, half, LANES)),
            bf16((number, half, LANES)),
            pltpu.VMEM((8, LANES), jnp.float32),
            pltpu.VMEM((4, 4, 8, LANES), jnp.float32),
            bf16((EARLY, 2, SIDE, rows, max(c[1] for c in CHUNKS[:EARLY]) * LANES)),
            pltpu.SemaphoreType.DMA((9 + EARLY,)),
            pltpu.SemaphoreType.DMA((len(CHUNKS) + 1,)),
            pltpu.SemaphoreType.DMA((RECEIVES,)),
        ],
        compiler_params=pltpu.CompilerParams(
            collective_id=0, has_side_effects=True, vmem_limit_bytes=24 * 2**20
        ),
        name="outer_step",
    )(*(pltpu.with_memory_space_constraint(a, pltpu.HBM) for a in (base, local, momentum)))
    hbm = pl.BlockSpec(memory_space=pltpu.HBM)
    new_params, new_momentum, rms = pl.pallas_call(
        write_out,
        out_shape=(
            pltpu.HBM((rows, columns), jnp.bfloat16),
            pltpu.HBM((rows, piece), jnp.float32),
            pltpu.HBM((1, 1), jnp.float32),
        ),
        in_specs=[vmem] * 3,
        out_specs=(hbm,) * 3,
        scratch_shapes=[pltpu.SemaphoreType.DMA((2 * SPLIT + 1,))],
        compiler_params=pltpu.CompilerParams(vmem_limit_bytes=2**20),
        name="write_out",
    )(*(pltpu.with_memory_space_constraint(a, pltpu.VMEM) for a in (new_params, new_momentum, rms)))
    return (new_params, new_momentum, rms[0, 0])


def solution(mesh):
    return jax.shard_map(
        per_device,
        mesh=mesh,
        in_specs=(P("fsdp", None), P("replica", "fsdp", None), P("fsdp", "replica")),
        out_specs=(P("fsdp", None), P("fsdp", "replica"), P()),
        check_vma=False,
    )
```

```python
import functools

import jax
import jax.numpy as jnp
from jax import lax
from jax.experimental import pallas as pl
from jax.experimental.pallas import tpu as pltpu
from jax.sharding import PartitionSpec as P

MESH = pl.DeviceIdType.MESH
LANES = 128
SIDE = 4
outer_rate = 0.7
momentum_decay = 0.9

CHUNKS = (
    (0, 2, "x"),
    (11, 1, "z"),
    (2, 2, "x"),
    (12, 1, "z"),
    (4, 2, "x"),
    (13, 1, "z"),
    (6, 2, "x"),
    (8, 2, "x"),
    (10, 1, "x"),
)
ORDER = (
    ("E2", 0), ("Sp", 0), ("E2", 1), ("E2", 6), ("E2", 4), ("Sp", 1), ("Sp", 4), ("Sp", 6), ("E1l", 4), ("E1r", 4), ("E2", 5), ("Swl", 4), ("Swr", 4),
    ("Sp", 5), ("E2", 3), ("E2", 2), ("E1r", 3), ("E2", 8), ("Sp", 2), ("Sp", 3), ("E1l", 1), ("E1r", 1), ("Swl", 1), ("Swr", 3), ("E0", 4),
    ("Swr", 1), ("E1l", 3), ("A2l", 4), ("A2r", 4), ("A2l", 1), ("E1l", 5), ("E1r", 6), ("E1l", 6), ("A2l", 6), ("Swr", 6), ("Swl", 5), ("A2r", 6),
    ("Swl", 3), ("Swl", 6), ("A2r", 1), ("E1r", 0), ("Swr", 0), ("E1r", 5), ("Swr", 5), ("A2r", 0), ("E0", 6), ("E1l", 0), ("E1l", 2), ("Swl", 0),
    ("R3a", 4), ("A2l", 0), ("R3b", 4), ("A2r", 3), ("Sp", 8), ("Swl", 2), ("A2l", 3), ("E1r", 2), ("E1r", 7), ("E0", 3), ("Swr", 2), ("R3c", 4),
    ("A2l", 2), ("E1r", 8), ("R3a", 6), ("A2r", 5), ("E0", 1), ("A2l", 5), ("E2", 7), ("A2r", 2), ("R4l", 4), ("E1l", 8), ("R4r", 4), ("E0", 0),
    ("R3a", 0), ("Sp", 7), ("Swl", 8), ("R3b", 6), ("R3b", 0), ("A2r", 8), ("R3c", 0), ("E1l", 7), ("E0", 2), ("Swr", 8), ("A2l", 8), ("Swr", 7),
    ("R4l", 6), ("E0", 8), ("R4r", 6), ("E0", 5), ("Swl", 7), ("R3a", 2), ("R5", 4), ("R4l", 0), ("A2l", 7), ("A2r", 7), ("R4r", 0), ("R3b", 2),
    ("R3a", 5), ("E0", 7), ("R3c", 6), ("R3a", 1), ("R3a", 3), ("R3a", 8), ("R5", 6), ("G8r", 4, 0), ("R4r", 2), ("R3c", 2), ("R3b", 3), ("R4l", 2),
    ("R3c", 8), ("R3b", 1), ("R3c", 3), ("R3b", 5), ("R3b", 8), ("R3a", 7), ("G6r", 4), ("G6l", 4), ("R4r", 3), ("R5", 0), ("G8l", 6, 0), ("R4l", 5),
    ("R4r", 8), ("R4r", 5), ("G8r", 6, 0), ("R4l", 8), ("G8l", 4, 0), ("R3c", 7), ("R3b", 7), ("R4l", 1), ("R4r", 1), ("R4l", 3), ("R5", 2),
    ("G8r", 4, -1), ("R4l", 7), ("G6l", 6), ("R4r", 7), ("G8l", 4, -1), ("G7", 4), ("G6r", 6), ("G8r", 0, 0), ("R5", 8), ("R5", 3), ("G6l", 0),
    ("G6r", 0), ("G8l", 6, 1), ("R3c", 1), ("R5", 1), ("R3c", 5), ("G8r", 6, 1), ("R5", 7), ("R5", 5), ("N0", 0), ("G6r", 2), ("G8l", 8, 0),
    ("G6r", 8), ("G6l", 3), ("G8r", 4, 2), ("G6l", 2), ("G6l", 8), ("G6r", 1), ("G7", 0), ("G8r", 8, 0), ("G8l", 7, 0), ("G6l", 1), ("G6r", 3),
    ("G8r", 0, 1), ("G6l", 7), ("N1", 0), ("G6r", 7), ("G6r", 5), ("G6l", 5), ("G8l", 2, 0), ("G7", 6), ("G8r", 7, 0), ("G8l", 6, -1), ("G8r", 2, 0),
    ("G8r", 2, 1), ("G8l", 0, -1), ("G8l", 4, 1), ("G8l", 8, 1), ("G7", 2), ("G7", 8), ("G8l", 0, 2), ("G8r", 8, -1), ("G7", 1), ("G7", 3),
    ("G8l", 1, -1), ("G8r", 0, -1), ("G8r", 2, -1), ("G8r", 0, 2), ("G8l", 0, 1), ("G8r", 7, 1), ("G8l", 2, -1), ("G8r", 3, -1), ("G7", 5),
    ("G8r", 1, 0), ("G8l", 3, 0), ("G8l", 1, 1), ("G8r", 3, 1), ("G7", 7), ("G8r", 8, 1), ("G8r", 4, 1), ("G8l", 3, 1), ("G8r", 3, 0), ("G8l", 4, 2),
    ("G8l", 2, 1), ("G8r", 1, 1), ("G8l", 1, 0), ("N2", 0), ("G8l", 3, -1), ("G8l", 7, -1), ("G8r", 1, -1), ("G8l", 0, 0), ("G8r", 6, -1),
    ("G8r", 6, 2), ("G8l", 8, -1), ("G8l", 1, 2), ("G8l", 5, 1), ("G8r", 1, 2), ("G8r", 7, -1), ("G8r", 5, -1), ("G8r", 5, 0), ("G8l", 5, 0),
    ("G8l", 6, 2), ("G8l", 3, 2), ("G8l", 2, 2), ("G8r", 3, 2), ("G8l", 8, 2), ("G8r", 2, 2), ("G8l", 5, -1), ("G8r", 5, 1), ("G8r", 8, 2),
    ("G8l", 5, 2), ("G8r", 5, 2), ("G8l", 7, 1), ("G8r", 7, 2), ("G8l", 7, 2), ("N3", 0), ("G9", 0), ("G9", 1), ("G9", 4), ("G9", 6), ("G9", 8),
    ("G9", 2), ("G9", 3), ("G9", 7), ("G9", 5),
)


def kernel(
    base_hbm, local_hbm, momentum_hbm, params_ref, new_momentum_ref, rms_ref,
    base_ref, local_ref, momentum_ref, coded_ref,
    full_l, full_r, half_l, half_r, last_l, last_r, part_l, part_r,
    squares_ref, norm_ref, early_ref, load_sem, send_sem, recv_sem,
):
    rows, columns = base_ref.shape
    half = rows // 2
    piece = columns // (SIDE * SIDE)
    replica = lax.axis_index("replica")
    fsdp = lax.axis_index("fsdp")
    at = {"x": replica // SIDE, "z": replica % SIDE}
    near, z_lo = fsdp % 2, fsdp // 8
    y = (fsdp // 2) % 4

    def shifted(axis, step):
        return (at[axis] + step + SIDE) % SIDE

    def device(axis, step):
        x, z = at["x"], at["z"]
        if axis == "x":
            x = shifted("x", step)
        else:
            z = shifted("z", step)
        return (x * SIDE + z, fsdp)

    def fsdp_device(axis, step):
        if axis == "y":
            return (replica, z_lo * 8 + (y + step) % 4 * 2 + near)
        other = (z_lo * 2 + near + step) % 4
        return (replica, other // 2 * 8 + y * 2 + other % 2)

    barrier = pltpu.get_barrier_semaphore()
    peers = [device(axis, step) for axis in ("x", "z") for step in (1, 2, 3)]
    peers += [fsdp_device(axis, step) for axis in ("y", "other") for step in (1, 2, 3)]
    for peer in peers:
        pl.semaphore_signal(barrier, inc=1, device_id=peer, device_id_type=MESH)

    for c, (start, count, first) in enumerate(CHUNKS[:EARLY]):
        for s in range(SIDE):
            x, z = (shifted("x", 2), s) if first == "x" else (s, shifted("z", 2))
            cols = pl.ds(pl.multiple_of((x * SIDE + z) * piece + start * LANES, LANES), count * LANES)
            for i, src in enumerate((base_hbm.at[:, cols], local_hbm.at[0, :, cols])):
                dst = early_ref.at[c, i, s, :, pl.ds(0, count * LANES)]
                pltpu.make_async_copy(src, dst, load_sem.at[9 + c]).start()

    group = SIDE * piece
    loads = {}
    for i, step in enumerate((2, 1, -1, 0)):
        cols = pl.ds(pl.multiple_of(shifted("x", step) * group, LANES), group)
        loads[step] = (
            pltpu.make_async_copy(base_hbm.at[:, cols], base_ref.at[:, cols], load_sem.at[2 * i]),
            pltpu.make_async_copy(local_hbm.at[0, :, cols], local_ref.at[:, cols], load_sem.at[2 * i + 1]),
        )
        for copy in loads[step]:
            copy.start()
    momentum_load = pltpu.make_async_copy(momentum_hbm, momentum_ref, load_sem.at[8])
    momentum_load.start()
    entered = []
    waited = set()
    squares_ref[...] = jnp.zeros_like(squares_ref)

    def loaded(step):
        if step not in waited:
            waited.add(step)
            for copy in loads[step]:
                copy.wait()

    groups = {}

    def slot(key):
        if key[:2] == ("G", 0):
            return ("p", key[-1])
        return (REUSED.get(key[0], key[0]), *key[1:])

    def send(key, src, dst, target):
        if not entered:
            entered.append(True)
            pl.semaphore_wait(barrier, len(peers))
        together = key
        if key[0] in GROUP:
            together = (GROUP[key[0]], key[-1])
        elif key[0] in ("G_r", "G_l"):
            together = ("G", *key[1:])
        i = groups.setdefault(slot(together), len(groups))
        pltpu.make_async_remote_copy(
            src_ref=src, dst_ref=dst, send_sem=send_sem.at[key[-1]], recv_sem=recv_sem.at[i],
            device_id=target, device_id_type=MESH,
        ).start()

    def wait(sem, sized):
        pltpu.make_async_copy(sized, sized, sem).wait()

    def recv(key, sized):
        if key not in waited:
            waited.add(key)
            wait(recv_sem.at[groups[slot(key)]], sized)

    def pieces(count, x, z):
        return coded_ref.at[pl.ds(0, count), pl.ds(0, x), pl.ds(0, z)]

    low, high, every = pl.ds(0, half), pl.ds(half, half), pl.ds(0, rows)

    def column(x, z, block):
        return pl.multiple_of((x * SIDE + z) * piece + block * LANES, LANES)

    def code_block(block, x, z):
        cols = pl.ds(column(x, z, block), LANES)
        code_values(block, x, z, base_ref[:, cols], local_ref[:, cols])

    def code_values(block, x, z, base, local):
        delta = base.astype(jnp.float32) - local.astype(jnp.float32)
        largest = jnp.max(jnp.abs(delta), axis=1, keepdims=True)
        scale = ((largest + 1e-06) * (1.0 / 448.0)).astype(jnp.bfloat16).astype(jnp.float32)
        coded = (delta * (1.0 / scale)).astype(jnp.bfloat16).astype(jnp.float32)
        coded_ref[block, x, z] = (coded * scale).astype(jnp.bfloat16)

    def over(start, count, body, unroll=2):
        def step(i, carry):
            body(start + i // SIDE, i % SIDE)
            return carry
        lax.fori_loop(0, count * SIDE, step, 0, unroll=unroll)

    def blocks(start, count, body):
        def step(i, carry):
            body(start + i)
            return carry
        lax.fori_loop(0, count, step, 0)

    def f32(value):
        return value.astype(jnp.float32)

    steps = {}
    for c, (start, count, first) in enumerate(CHUNKS):
        second = "z" if first == "x" else "x"
        ks = pl.ds(start, count)

        def xz(f, s, first=first):
            return (f, s) if first == "x" else (s, f)

        def row_of(f, rs, ks=ks, first=first):
            if first == "x":
                return coded_ref.at[ks, f, :, rs]
            return coded_ref.at[ks, :, f, rs]

        def piece_of(f, s, rs, ks=ks, xz=xz):
            return coded_ref.at[(ks, *xz(f, s), rs)]

        def gathered(f, s, rs, start=start, count=count, xz=xz):
            return params_ref.at[rs, pl.ds(column(*xz(f, s), start), count * LANES)]

        def code(f_step, start=start, count=count, first=first, xz=xz):
            if first == "x":
                loaded(f_step)
            else:
                for step in (2, 1, -1, 0):
                    loaded(step)
            f = shifted(first, f_step)
            over(start, count, lambda block, s: code_block(block, *xz(f, s)))


        def E2(c=c, start=start, count=count, first=first, code=code, xz=xz):
            if c >= EARLY:
                code(2)
                return
            wait(load_sem.at[9 + c], early_ref.at[c, :, :, :, pl.ds(0, count * LANES)])
            f = shifted(first, 2)

            def early(block, s):
                cols = pl.ds(pl.multiple_of((block - start) * LANES, LANES), LANES)
                code_values(block, *xz(f, s), early_ref[c, 0, s, :, cols], early_ref[c, 1, s, :, cols])
            over(start, count, early)

        def E1r(code=code):
            code(1)

        def E1l(code=code):
            code(-1)

        def E0(code=code):
            code(0)

        def Sp(c=c, ks=ks, first=first, row_of=row_of):
            far = shifted(first, 2)
            send(("p_r", c), row_of(far, low), half_l.at[ks], device(first, 1))
            send(("p_l", c), row_of(far, high), half_r.at[ks], device(first, -1))

        def Swr(c=c, ks=ks, first=first, row_of=row_of):
            send(("w_r", c), row_of(shifted(first, 1), high), full_l.at[ks, :, high], device(first, 1))

        def Swl(c=c, ks=ks, first=first, row_of=row_of):
            send(("w_l", c), row_of(shifted(first, -1), low), full_r.at[ks, :, low], device(first, -1))

        def join(name, step, rs, got, into, c=c, ks=ks, start=start, count=count, first=first, row_of=row_of, xz=xz):
            f = shifted(first, step)
            recv(("p", c), pieces(count, 4, 1))

            def add(block, s):
                index = (block, *xz(f, s), rs)
                coded_ref[index] = (f32(coded_ref[index]) + f32(got[block, s])).astype(jnp.bfloat16)
            over(start, count, add, unroll=4)
            send(("s_" + name, c), row_of(f, rs), into.at[ks, :, rs], device(first, step))

        def A2r(join=join):
            join("r", 1, low, half_l, full_l)

        def A2l(join=join):
            join("l", -1, high, half_r, full_r)

        def total_at(s, start=start, count=count, first=first, xz=xz):
            def add(block):
                index = (block, *xz(at[first], s))
                total = f32(coded_ref[index]) + f32(full_l[block, s]) + f32(full_r[block, s])
                coded_ref[index] = total.astype(jnp.bfloat16)
            blocks(start, count, add)

        def R3a(c=c, ks=ks, count=count, first=first, second=second, piece_of=piece_of, total_at=total_at):
            recv(("first", c), pieces(count, 4, 2))
            far = shifted(second, 2)
            total_at(far)
            send(("P_r", c), piece_of(at[first], far, low), part_l.at[ks], device(second, 1))
            send(("P_l", c), piece_of(at[first], far, high), part_r.at[ks], device(second, -1))

        def R3b(c=c, ks=ks, first=first, second=second, piece_of=piece_of, total_at=total_at):
            for name, step, rs, into in (("r", 1, high, last_l), ("l", -1, low, last_r)):
                s = shifted(second, step)
                total_at(s)
                send(("W_" + name, c), piece_of(at[first], s, rs), into.at[ks, rs], device(second, step))

        def R3c(second=second, total_at=total_at):
            total_at(at[second])

        def last_join(name, step, rs, got, into, c=c, ks=ks, start=start, count=count, first=first, second=second,
                      piece_of=piece_of, xz=xz):
            s = shifted(second, step)
            recv(("P", c), pieces(count, 1, 1))

            def add(block):
                index = (block, *xz(at[first], s), rs)
                coded_ref[index] = (f32(coded_ref[index]) + f32(got[block])).astype(jnp.bfloat16)
            blocks(start, count, add)
            send(("S_" + name, c), piece_of(at[first], s, rs), into.at[ks, rs], device(second, step))

        def R4r(last_join=last_join):
            last_join("r", 1, low, part_l, last_l)

        def R4l(last_join=last_join):
            last_join("l", -1, high, part_r, last_r)

        def spread(s, c=c, first=first, second=second, gathered=gathered):
            for name, step in (("r", 1), ("l", -1)):
                part = gathered(at[first], shifted(second, s), every)
                send(("G_" + name, s, c), part, part, device(first, step))

        def R5(c=c, start=start, count=count, first=first, second=second, gathered=gathered, spread=spread):
            recv(("second", c), pieces(count, 1, 2))
            if "momentum" not in waited:
                waited.add("momentum")
                momentum_load.wait()

            def update(block):
                x, z = at["x"], at["z"]
                total = f32(coded_ref[block, x, z]) + f32(last_l[block]) + f32(last_r[block])
                grad = total * (1.0 / (SIDE * SIDE))
                squares_ref[...] += jnp.sum((grad * grad).reshape(rows // 8, 8, LANES), axis=0)
                own = pl.ds(pl.multiple_of(block * LANES, LANES), LANES)
                new_momentum = momentum_decay * momentum_ref[:, own] + grad
                new_momentum_ref[:, own] = new_momentum
                cols = pl.ds(column(x, z, block), LANES)
                stepped = f32(base_ref[:, cols]) - outer_rate * (momentum_decay * new_momentum + grad)
                params_ref[:, cols] = stepped.astype(jnp.bfloat16)
            blocks(start, count, update)
            mine = gathered(at[first], at[second], every)
            send(("g_r", c), mine, mine, device(second, 1))
            send(("g_l", c), mine, mine, device(second, -1))
            spread(0)

        def pass_on(name, step, rs, c=c, count=count, first=first, second=second, gathered=gathered, spread=spread):
            recv(("g", c), pieces(count, 1, 2))
            passed = gathered(at[first], shifted(second, -step), rs)
            send(("h_" + name, c), passed, passed, device(second, step))
            spread(-step)

        def G6r(pass_on=pass_on):
            pass_on("r", 1, low)

        def G6l(pass_on=pass_on):
            pass_on("l", -1, high)

        def G7(c=c, count=count, spread=spread):
            recv(("far", c), pieces(count, 1, 1))
            spread(2)

        def last_pass(s, name, step, rs, c=c, count=count, first=first, second=second, gathered=gathered):
            recv(("G", s, c), pieces(count, 1, 2))
            passed = gathered(shifted(first, -step), shifted(second, s), rs)
            send(("H_" + name, s, c), passed, passed, device(first, step))

        def G9(c=c, count=count):
            recv(("last", c), pieces(count, 4, 1))

        for step in (E2, E1r, E1l, E0, Sp, Swr, Swl, A2r, A2l, R3a, R3b, R3c, R4r, R4l, R5, G6r, G6l, G7, G9):
            steps[step.__name__, c] = step
        for s in (0, 1, -1, 2):
            steps["G8r", c, s] = functools.partial(last_pass, s, "r", 1, low)
            steps["G8l", c, s] = functools.partial(last_pass, s, "l", -1, high)

    def norm_round(i, place, target):
        for step in (1, 2, 3):
            send((f"n{i}", len(CHUNKS)), norm_ref.at[i, place], norm_ref.at[i, place], target(step))

    def norm_sum(i):
        recv((f"n{i}", len(CHUNKS)), norm_ref.at[0, pl.ds(0, 3)])
        return norm_ref[i, 0] + norm_ref[i, 1] + norm_ref[i, 2] + norm_ref[i, 3]

    other = z_lo * 2 + near

    def N0():
        norm_ref[0, at["x"]] = squares_ref[...]
        norm_round(0, at["x"], lambda step: device("x", step))

    def N1():
        norm_ref[1, at["z"]] = norm_sum(0)
        norm_round(1, at["z"], lambda step: device("z", step))

    def N2():
        norm_ref[2, y] = norm_sum(1)
        norm_round(2, y, lambda step: fsdp_device("y", step))

    def N3():
        norm_ref[3, other] = norm_sum(2)
        norm_round(3, other, lambda step: fsdp_device("other", step))

    for step in (N0, N1, N2, N3):
        steps[step.__name__, 0] = step

    for key in ORDER[:-len(CHUNKS)]:
        steps[key]()
    total = jnp.sum(norm_sum(3), axis=(0, 1), keepdims=True)
    entries = rows * columns * 16
    rms_ref[...] = jnp.broadcast_to(jnp.sqrt(total / entries), rms_ref.shape)
    for key in ORDER[-len(CHUNKS):]:
        steps[key]()
    for c, (_, count, _) in enumerate(CHUNKS):
        wide, high_, deep = SENT[count]
        wait(send_sem.at[c], coded_ref.at[pl.ds(0, wide), pl.ds(0, high_), pl.ds(0, deep)])
    wait(send_sem.at[len(CHUNKS)], norm_ref.at[pl.ds(0, 3)])


second_of = {"x": "z", "z": "x"}
SPLIT = 1
EARLY = 2
RECEIVES = len(CHUNKS) * 7 + 4
REUSED = {"g": "P", "last": "first", "far": "second"}
GROUP = {
    "p_r": "p", "p_l": "p", "P_r": "P", "P_l": "P", "g_r": "g", "g_l": "g",
    "w_r": "first", "w_l": "first", "s_r": "first", "s_l": "first",
    "W_r": "second", "W_l": "second", "S_r": "second", "S_l": "second",
    "h_r": "far", "h_l": "far", "H_r": "last", "H_l": "last",
}
SENT = {1: (10, 3, 1), 2: (5, 4, 3), 3: (10, 3, 3), 4: (10, 4, 3)}


def write_out(params_ref, momentum_ref, rms_ref, params_hbm, momentum_hbm, rms_hbm, sem):
    copies = [pltpu.make_async_copy(rms_ref, rms_hbm, sem.at[0])]
    for src, dst in ((params_ref, params_hbm), (momentum_ref, momentum_hbm)):
        step = src.shape[0] // SPLIT
        for i in range(SPLIT):
            part = pl.ds(i * step, step)
            copies.append(pltpu.make_async_copy(src.at[part], dst.at[part], sem.at[len(copies)]))
    for copy in copies:
        copy.start()
    for copy in copies:
        copy.wait()


def per_device(base, local, momentum):
    rows, columns = base.shape
    piece = columns // (SIDE * SIDE)
    number = piece // LANES
    half = rows // 2
    bf16 = functools.partial(pltpu.VMEM, dtype=jnp.bfloat16)
    vmem = pl.BlockSpec(memory_space=pltpu.VMEM)
    new_params, new_momentum, rms = pl.pallas_call(
        kernel,
        out_shape=(
            pltpu.VMEM((rows, columns), jnp.bfloat16),
            pltpu.VMEM((rows, piece), jnp.float32),
            pltpu.VMEM((1, 1), jnp.float32),
        ),
        in_specs=[pl.BlockSpec(memory_space=pltpu.HBM)] * 3,
        out_specs=(vmem, vmem, vmem),
        scratch_shapes=[
            bf16((rows, columns)),
            bf16((rows, columns)),
            pltpu.VMEM((rows, piece), jnp.float32),
            bf16((number, SIDE, SIDE, rows, LANES)),
            bf16((number, SIDE, rows, LANES)),
            bf16((number, SIDE, rows, LANES)),
            bf16((number, SIDE, half, LANES)),
            bf16((number, SIDE, half, LANES)),
            bf16((number, rows, LANES)),
            bf16((number, rows, LANES)),
            bf16((number, half, LANES)),
            bf16((number, half, LANES)),
            pltpu.VMEM((8, LANES), jnp.float32),
            pltpu.VMEM((4, 4, 8, LANES), jnp.float32),
            bf16((EARLY, 2, SIDE, rows, max(c[1] for c in CHUNKS[:EARLY]) * LANES)),
            pltpu.SemaphoreType.DMA((9 + EARLY,)),
            pltpu.SemaphoreType.DMA((len(CHUNKS) + 1,)),
            pltpu.SemaphoreType.DMA((RECEIVES,)),
        ],
        compiler_params=pltpu.CompilerParams(
            collective_id=0, has_side_effects=True, vmem_limit_bytes=24 * 2**20
        ),
        name="outer_step",
    )(*(pltpu.with_memory_space_constraint(a, pltpu.HBM) for a in (base, local, momentum)))
    hbm = pl.BlockSpec(memory_space=pltpu.HBM)
    new_params, new_momentum, rms = pl.pallas_call(
        write_out,
        out_shape=(
            pltpu.HBM((rows, columns), jnp.bfloat16),
            pltpu.HBM((rows, piece), jnp.float32),
            pltpu.HBM((1, 1), jnp.float32),
        ),
        in_specs=[vmem] * 3,
        out_specs=(hbm,) * 3,
        scratch_shapes=[pltpu.SemaphoreType.DMA((2 * SPLIT + 1,))],
        compiler_params=pltpu.CompilerParams(vmem_limit_bytes=2**20),
        name="write_out",
    )(*(pltpu.with_memory_space_constraint(a, pltpu.VMEM) for a in (new_params, new_momentum, rms)))
    return (new_params, new_momentum, rms[0, 0])


def solution(mesh):
    return jax.shard_map(
        per_device,
        mesh=mesh,
        in_specs=(P("fsdp", None), P("replica", "fsdp", None), P("fsdp", "replica")),
        out_specs=(P("fsdp", None), P("fsdp", "replica"), P()),
        check_vma=False,
    )
```

```python
import functools

import jax
import jax.numpy as jnp
from jax import lax
from jax.experimental import pallas as pl
from jax.experimental.pallas import tpu as pltpu
from jax.sharding import PartitionSpec as P

MESH = pl.DeviceIdType.MESH
LANES = 128
SIDE = 4
outer_rate = 0.7
momentum_decay = 0.9

CHUNKS = (
    (0, 2, "x"),
    (11, 1, "z"),
    (2, 2, "x"),
    (12, 1, "z"),
    (4, 2, "x"),
    (13, 1, "z"),
    (6, 2, "x"),
    (8, 2, "x"),
    (10, 1, "x"),
)
ORDER = (
    ("E2", 0), ("Sp", 0), ("E2", 1), ("E2", 6), ("E2", 4), ("Sp", 1), ("Sp", 4), ("Sp", 6), ("E1l", 4), ("E1r", 4), ("E2", 5), ("Swl", 4), ("Swr", 4),
    ("Sp", 5), ("E2", 3), ("E2", 2), ("E1r", 3), ("E2", 8), ("Sp", 2), ("Sp", 3), ("E1l", 1), ("E1r", 1), ("Swl", 1), ("Swr", 3), ("E0", 4),
    ("Swr", 1), ("E1l", 3), ("A2l", 4), ("A2r", 4), ("A2l", 1), ("E1l", 5), ("E1r", 6), ("E1l", 6), ("A2l", 6), ("Swr", 6), ("Swl", 5), ("A2r", 6),
    ("Swl", 3), ("Swl", 6), ("A2r", 1), ("E1r", 0), ("Swr", 0), ("E1r", 5), ("Swr", 5), ("A2r", 0), ("E0", 6), ("E1l", 0), ("E1l", 2), ("Swl", 0),
    ("R3a", 4), ("A2l", 0), ("R3b", 4), ("A2r", 3), ("Sp", 8), ("Swl", 2), ("A2l", 3), ("E1r", 2), ("E1r", 7), ("E0", 3), ("Swr", 2), ("R3c", 4),
    ("A2l", 2), ("E1r", 8), ("R3a", 6), ("A2r", 5), ("E0", 1), ("A2l", 5), ("E2", 7), ("A2r", 2), ("R4l", 4), ("E1l", 8), ("R4r", 4), ("E0", 0),
    ("R3a", 0), ("Sp", 7), ("Swl", 8), ("R3b", 6), ("R3b", 0), ("A2r", 8), ("R3c", 0), ("E1l", 7), ("E0", 2), ("Swr", 8), ("A2l", 8), ("Swr", 7),
    ("R4l", 6), ("E0", 8), ("R4r", 6), ("E0", 5), ("Swl", 7), ("R3a", 2), ("R5", 4), ("R4l", 0), ("A2l", 7), ("A2r", 7), ("R4r", 0), ("R3b", 2),
    ("R3a", 5), ("E0", 7), ("R3c", 6), ("R3a", 1), ("R3a", 3), ("R3a", 8), ("R5", 6), ("G8r", 4, 0), ("R4r", 2), ("R3c", 2), ("R3b", 3), ("R4l", 2),
    ("R3c", 8), ("R3b", 1), ("R3c", 3), ("R3b", 5), ("R3b", 8), ("R3a", 7), ("G6r", 4), ("G6l", 4), ("R4r", 3), ("R5", 0), ("G8l", 6, 0), ("R4l", 5),
    ("R4r", 8), ("R4r", 5), ("G8r", 6, 0), ("R4l", 8), ("G8l", 4, 0), ("R3c", 7), ("R3b", 7), ("R4l", 1), ("R4r", 1), ("R4l", 3), ("R5", 2),
    ("G8r", 4, -1), ("R4l", 7), ("G6l", 6), ("R4r", 7), ("G8l", 4, -1), ("G7", 4), ("G6r", 6), ("G8r", 0, 0), ("R5", 8), ("R5", 3), ("G6l", 0),
    ("G6r", 0), ("G8l", 6, 1), ("R3c", 1), ("R5", 1), ("R3c", 5), ("G8r", 6, 1), ("R5", 7), ("R5", 5), ("N0", 0), ("G6r", 2), ("G8l", 8, 0),
    ("G6r", 8), ("G6l", 3), ("G8r", 4, 2), ("G6l", 2), ("G6l", 8), ("G6r", 1), ("G7", 0), ("G8r", 8, 0), ("G8l", 7, 0), ("G6l", 1), ("G6r", 3),
    ("G8r", 0, 1), ("G6l", 7), ("N1", 0), ("G6r", 7), ("G6r", 5), ("G6l", 5), ("G8l", 2, 0), ("G7", 6), ("G8r", 7, 0), ("G8l", 6, -1), ("G8r", 2, 0),
    ("G8r", 2, 1), ("G8l", 0, -1), ("G8l", 4, 1), ("G8l", 8, 1), ("G7", 2), ("G7", 8), ("G8l", 0, 2), ("G8r", 8, -1), ("G7", 1), ("G7", 3),
    ("G8l", 1, -1), ("G8r", 0, -1), ("G8r", 2, -1), ("G8r", 0, 2), ("G8l", 0, 1), ("G8r", 7, 1), ("G8l", 2, -1), ("G8r", 3, -1), ("G7", 5),
    ("G8r", 1, 0), ("G8l", 3, 0), ("G8l", 1, 1), ("G8r", 3, 1), ("G7", 7), ("G8r", 8, 1), ("G8r", 4, 1), ("G8l", 3, 1), ("G8r", 3, 0), ("G8l", 4, 2),
    ("G8l", 2, 1), ("G8r", 1, 1), ("G8l", 1, 0), ("N2", 0), ("G8l", 3, -1), ("G8l", 7, -1), ("G8r", 1, -1), ("G8l", 0, 0), ("G8r", 6, -1),
    ("G8r", 6, 2), ("G8l", 8, -1), ("G8l", 1, 2), ("G8l", 5, 1), ("G8r", 1, 2), ("G8r", 7, -1), ("G8r", 5, -1), ("G8r", 5, 0), ("G8l", 5, 0),
    ("G8l", 6, 2), ("G8l", 3, 2), ("G8l", 2, 2), ("G8r", 3, 2), ("G8l", 8, 2), ("G8r", 2, 2), ("G8l", 5, -1), ("G8r", 5, 1), ("G8r", 8, 2),
    ("G8l", 5, 2), ("G8r", 5, 2), ("G8l", 7, 1), ("G8r", 7, 2), ("G8l", 7, 2), ("N3", 0), ("G9", 0), ("G9", 1), ("G9", 4), ("G9", 6), ("G9", 8),
    ("G9", 2), ("G9", 3), ("G9", 7), ("G9", 5),
)


def kernel(
    base_hbm, local_hbm, momentum_hbm, params_ref, new_momentum_ref, rms_ref,
    base_ref, local_ref, momentum_ref, coded_ref,
    full_l, full_r, half_l, half_r, last_l, last_r, part_l, part_r,
    squares_ref, norm_ref, early_ref, load_sem, send_sem, recv_sem,
):
    rows, columns = base_ref.shape
    half = rows // 2
    piece = columns // (SIDE * SIDE)
    replica = lax.axis_index("replica")
    fsdp = lax.axis_index("fsdp")
    at = {"x": replica // SIDE, "z": replica % SIDE}
    near, z_lo = fsdp % 2, fsdp // 8
    y = (fsdp // 2) % 4

    def shifted(axis, step):
        return (at[axis] + step + SIDE) % SIDE

    def device(axis, step):
        x, z = at["x"], at["z"]
        if axis == "x":
            x = shifted("x", step)
        else:
            z = shifted("z", step)
        return (x * SIDE + z, fsdp)

    def fsdp_device(axis, step):
        if axis == "y":
            return (replica, z_lo * 8 + (y + step) % 4 * 2 + near)
        other = (z_lo * 2 + near + step) % 4
        return (replica, other // 2 * 8 + y * 2 + other % 2)

    barrier = pltpu.get_barrier_semaphore()
    peers = [device(axis, step) for axis in ("x", "z") for step in (1, 2, 3)]
    peers += [fsdp_device(axis, step) for axis in ("y", "other") for step in (1, 2, 3)]
    for peer in peers:
        pl.semaphore_signal(barrier, inc=1, device_id=peer, device_id_type=MESH)

    for c, (start, count, first) in enumerate(CHUNKS[:EARLY]):
        for s in range(SIDE):
            x, z = (shifted("x", 2), s) if first == "x" else (s, shifted("z", 2))
            cols = pl.ds(pl.multiple_of((x * SIDE + z) * piece + start * LANES, LANES), count * LANES)
            for i, src in enumerate((base_hbm.at[:, cols], local_hbm.at[0, :, cols])):
                dst = early_ref.at[c, i, s, :, pl.ds(0, count * LANES)]
                pltpu.make_async_copy(src, dst, load_sem.at[9 + c]).start()

    group = SIDE * piece
    loads = {}
    for i, step in enumerate((2, 1, -1, 0)):
        cols = pl.ds(pl.multiple_of(shifted("x", step) * group, LANES), group)
        loads[step] = (
            pltpu.make_async_copy(base_hbm.at[:, cols], base_ref.at[:, cols], load_sem.at[2 * i]),
            pltpu.make_async_copy(local_hbm.at[0, :, cols], local_ref.at[:, cols], load_sem.at[2 * i + 1]),
        )
        for copy in loads[step]:
            copy.start()
    momentum_load = pltpu.make_async_copy(momentum_hbm, momentum_ref, load_sem.at[8])
    momentum_load.start()
    entered = []
    waited = set()
    squares_ref[...] = jnp.zeros_like(squares_ref)

    def loaded(step):
        if step not in waited:
            waited.add(step)
            for copy in loads[step]:
                copy.wait()

    groups = {}

    def slot(key):
        if key[:2] == ("G", 0):
            return ("p", key[-1])
        return (REUSED.get(key[0], key[0]), *key[1:])

    def send(key, src, dst, target):
        if not entered:
            entered.append(True)
            pl.semaphore_wait(barrier, len(peers))
        together = key
        if key[0] in GROUP:
            together = (GROUP[key[0]], key[-1])
        elif key[0] in ("G_r", "G_l"):
            together = ("G", *key[1:])
        i = groups.setdefault(slot(together), len(groups))
        pltpu.make_async_remote_copy(
            src_ref=src, dst_ref=dst, send_sem=send_sem.at[key[-1]], recv_sem=recv_sem.at[i],
            device_id=target, device_id_type=MESH,
        ).start()

    def wait(sem, sized):
        pltpu.make_async_copy(sized, sized, sem).wait()

    def recv(key, sized):
        if key not in waited:
            waited.add(key)
            wait(recv_sem.at[groups[slot(key)]], sized)

    def pieces(count, x, z):
        return coded_ref.at[pl.ds(0, count), pl.ds(0, x), pl.ds(0, z)]

    low, high, every = pl.ds(0, half), pl.ds(half, half), pl.ds(0, rows)

    def column(x, z, block):
        return pl.multiple_of((x * SIDE + z) * piece + block * LANES, LANES)

    def code_block(block, x, z):
        cols = pl.ds(column(x, z, block), LANES)
        code_values(block, x, z, base_ref[:, cols], local_ref[:, cols])

    def code_values(block, x, z, base, local):
        delta = base.astype(jnp.float32) - local.astype(jnp.float32)
        largest = jnp.max(jnp.abs(delta), axis=1, keepdims=True)
        scale = ((largest + 1e-06) * (1.0 / 448.0)).astype(jnp.bfloat16).astype(jnp.float32)
        coded = (delta * (1.0 / scale)).astype(jnp.bfloat16).astype(jnp.float32)
        coded_ref[block, x, z] = (coded * scale).astype(jnp.bfloat16)

    def over(start, count, body, unroll=2):
        def step(i, carry):
            body(start + i // SIDE, i % SIDE)
            return carry
        lax.fori_loop(0, count * SIDE, step, 0, unroll=unroll)

    def blocks(start, count, body):
        def step(i, carry):
            body(start + i)
            return carry
        lax.fori_loop(0, count, step, 0)

    def f32(value):
        return value.astype(jnp.float32)

    steps = {}
    for c, (start, count, first) in enumerate(CHUNKS):
        second = "z" if first == "x" else "x"
        ks = pl.ds(start, count)

        def xz(f, s, first=first):
            return (f, s) if first == "x" else (s, f)

        def row_of(f, rs, ks=ks, first=first):
            if first == "x":
                return coded_ref.at[ks, f, :, rs]
            return coded_ref.at[ks, :, f, rs]

        def piece_of(f, s, rs, ks=ks, xz=xz):
            return coded_ref.at[(ks, *xz(f, s), rs)]

        def gathered(f, s, rs, start=start, count=count, xz=xz):
            return params_ref.at[rs, pl.ds(column(*xz(f, s), start), count * LANES)]

        def code(f_step, start=start, count=count, first=first, xz=xz):
            if first == "x":
                loaded(f_step)
            else:
                for step in (2, 1, -1, 0):
                    loaded(step)
            f = shifted(first, f_step)
            over(start, count, lambda block, s: code_block(block, *xz(f, s)))


        def E2(c=c, start=start, count=count, first=first, code=code, xz=xz):
            if c >= EARLY:
                code(2)
                return
            wait(load_sem.at[9 + c], early_ref.at[c, :, :, :, pl.ds(0, count * LANES)])
            f = shifted(first, 2)

            def early(block, s):
                cols = pl.ds(pl.multiple_of((block - start) * LANES, LANES), LANES)
                code_values(block, *xz(f, s), early_ref[c, 0, s, :, cols], early_ref[c, 1, s, :, cols])
            over(start, count, early, unroll=4)

        def E1r(code=code):
            code(1)

        def E1l(code=code):
            code(-1)

        def E0(code=code):
            code(0)

        def Sp(c=c, ks=ks, first=first, row_of=row_of):
            far = shifted(first, 2)
            send(("p_r", c), row_of(far, low), half_l.at[ks], device(first, 1))
            send(("p_l", c), row_of(far, high), half_r.at[ks], device(first, -1))

        def Swr(c=c, ks=ks, first=first, row_of=row_of):
            send(("w_r", c), row_of(shifted(first, 1), high), full_l.at[ks, :, high], device(first, 1))

        def Swl(c=c, ks=ks, first=first, row_of=row_of):
            send(("w_l", c), row_of(shifted(first, -1), low), full_r.at[ks, :, low], device(first, -1))

        def join(name, step, rs, got, into, c=c, ks=ks, start=start, count=count, first=first, row_of=row_of, xz=xz):
            f = shifted(first, step)
            recv(("p", c), pieces(count, 4, 1))

            def add(block, s):
                index = (block, *xz(f, s), rs)
                coded_ref[index] = (f32(coded_ref[index]) + f32(got[block, s])).astype(jnp.bfloat16)
            over(start, count, add, unroll=4)
            send(("s_" + name, c), row_of(f, rs), into.at[ks, :, rs], device(first, step))

        def A2r(join=join):
            join("r", 1, low, half_l, full_l)

        def A2l(join=join):
            join("l", -1, high, half_r, full_r)

        def total_at(s, start=start, count=count, first=first, xz=xz):
            def add(block):
                index = (block, *xz(at[first], s))
                total = f32(coded_ref[index]) + f32(full_l[block, s]) + f32(full_r[block, s])
                coded_ref[index] = total.astype(jnp.bfloat16)
            blocks(start, count, add)

        def R3a(c=c, ks=ks, count=count, first=first, second=second, piece_of=piece_of, total_at=total_at):
            recv(("first", c), pieces(count, 4, 2))
            far = shifted(second, 2)
            total_at(far)
            send(("P_r", c), piece_of(at[first], far, low), part_l.at[ks], device(second, 1))
            send(("P_l", c), piece_of(at[first], far, high), part_r.at[ks], device(second, -1))

        def R3b(c=c, ks=ks, first=first, second=second, piece_of=piece_of, total_at=total_at):
            for name, step, rs, into in (("r", 1, high, last_l), ("l", -1, low, last_r)):
                s = shifted(second, step)
                total_at(s)
                send(("W_" + name, c), piece_of(at[first], s, rs), into.at[ks, rs], device(second, step))

        def R3c(second=second, total_at=total_at):
            total_at(at[second])

        def last_join(name, step, rs, got, into, c=c, ks=ks, start=start, count=count, first=first, second=second,
                      piece_of=piece_of, xz=xz):
            s = shifted(second, step)
            recv(("P", c), pieces(count, 1, 1))

            def add(block):
                index = (block, *xz(at[first], s), rs)
                coded_ref[index] = (f32(coded_ref[index]) + f32(got[block])).astype(jnp.bfloat16)
            blocks(start, count, add)
            send(("S_" + name, c), piece_of(at[first], s, rs), into.at[ks, rs], device(second, step))

        def R4r(last_join=last_join):
            last_join("r", 1, low, part_l, last_l)

        def R4l(last_join=last_join):
            last_join("l", -1, high, part_r, last_r)

        def spread(s, c=c, first=first, second=second, gathered=gathered):
            for name, step in (("r", 1), ("l", -1)):
                part = gathered(at[first], shifted(second, s), every)
                send(("G_" + name, s, c), part, part, device(first, step))

        def R5(c=c, start=start, count=count, first=first, second=second, gathered=gathered, spread=spread):
            recv(("second", c), pieces(count, 1, 2))
            if "momentum" not in waited:
                waited.add("momentum")
                momentum_load.wait()

            def update(block):
                x, z = at["x"], at["z"]
                total = f32(coded_ref[block, x, z]) + f32(last_l[block]) + f32(last_r[block])
                grad = total * (1.0 / (SIDE * SIDE))
                squares_ref[...] += jnp.sum((grad * grad).reshape(rows // 8, 8, LANES), axis=0)
                own = pl.ds(pl.multiple_of(block * LANES, LANES), LANES)
                new_momentum = momentum_decay * momentum_ref[:, own] + grad
                new_momentum_ref[:, own] = new_momentum
                cols = pl.ds(column(x, z, block), LANES)
                stepped = f32(base_ref[:, cols]) - outer_rate * (momentum_decay * new_momentum + grad)
                params_ref[:, cols] = stepped.astype(jnp.bfloat16)
            blocks(start, count, update)
            mine = gathered(at[first], at[second], every)
            send(("g_r", c), mine, mine, device(second, 1))
            send(("g_l", c), mine, mine, device(second, -1))
            spread(0)

        def pass_on(name, step, rs, c=c, count=count, first=first, second=second, gathered=gathered, spread=spread):
            recv(("g", c), pieces(count, 1, 2))
            passed = gathered(at[first], shifted(second, -step), rs)
            send(("h_" + name, c), passed, passed, device(second, step))
            spread(-step)

        def G6r(pass_on=pass_on):
            pass_on("r", 1, low)

        def G6l(pass_on=pass_on):
            pass_on("l", -1, high)

        def G7(c=c, count=count, spread=spread):
            recv(("far", c), pieces(count, 1, 1))
            spread(2)

        def last_pass(s, name, step, rs, c=c, count=count, first=first, second=second, gathered=gathered):
            recv(("G", s, c), pieces(count, 1, 2))
            passed = gathered(shifted(first, -step), shifted(second, s), rs)
            send(("H_" + name, s, c), passed, passed, device(first, step))

        def G9(c=c, count=count):
            recv(("last", c), pieces(count, 4, 1))

        for step in (E2, E1r, E1l, E0, Sp, Swr, Swl, A2r, A2l, R3a, R3b, R3c, R4r, R4l, R5, G6r, G6l, G7, G9):
            steps[step.__name__, c] = step
        for s in (0, 1, -1, 2):
            steps["G8r", c, s] = functools.partial(last_pass, s, "r", 1, low)
            steps["G8l", c, s] = functools.partial(last_pass, s, "l", -1, high)

    def norm_round(i, place, target):
        for step in (1, 2, 3):
            send((f"n{i}", len(CHUNKS)), norm_ref.at[i, place], norm_ref.at[i, place], target(step))

    def norm_sum(i):
        recv((f"n{i}", len(CHUNKS)), norm_ref.at[0, pl.ds(0, 3)])
        return norm_ref[i, 0] + norm_ref[i, 1] + norm_ref[i, 2] + norm_ref[i, 3]

    other = z_lo * 2 + near

    def N0():
        norm_ref[0, at["x"]] = squares_ref[...]
        norm_round(0, at["x"], lambda step: device("x", step))

    def N1():
        norm_ref[1, at["z"]] = norm_sum(0)
        norm_round(1, at["z"], lambda step: device("z", step))

    def N2():
        norm_ref[2, y] = norm_sum(1)
        norm_round(2, y, lambda step: fsdp_device("y", step))

    def N3():
        norm_ref[3, other] = norm_sum(2)
        norm_round(3, other, lambda step: fsdp_device("other", step))

    for step in (N0, N1, N2, N3):
        steps[step.__name__, 0] = step

    for key in ORDER[:-len(CHUNKS)]:
        steps[key]()
    total = jnp.sum(norm_sum(3), axis=(0, 1), keepdims=True)
    entries = rows * columns * 16
    rms_ref[...] = jnp.broadcast_to(jnp.sqrt(total / entries), rms_ref.shape)
    for key in ORDER[-len(CHUNKS):]:
        steps[key]()
    for c, (_, count, _) in enumerate(CHUNKS):
        wide, high_, deep = SENT[count]
        wait(send_sem.at[c], coded_ref.at[pl.ds(0, wide), pl.ds(0, high_), pl.ds(0, deep)])
    wait(send_sem.at[len(CHUNKS)], norm_ref.at[pl.ds(0, 3)])


second_of = {"x": "z", "z": "x"}
SPLIT = 1
EARLY = 2
RECEIVES = len(CHUNKS) * 7 + 4
REUSED = {"g": "P", "last": "first", "far": "second"}
GROUP = {
    "p_r": "p", "p_l": "p", "P_r": "P", "P_l": "P", "g_r": "g", "g_l": "g",
    "w_r": "first", "w_l": "first", "s_r": "first", "s_l": "first",
    "W_r": "second", "W_l": "second", "S_r": "second", "S_l": "second",
    "h_r": "far", "h_l": "far", "H_r": "last", "H_l": "last",
}
SENT = {1: (10, 3, 1), 2: (5, 4, 3), 3: (10, 3, 3), 4: (10, 4, 3)}


def write_out(params_ref, momentum_ref, rms_ref, params_hbm, momentum_hbm, rms_hbm, sem):
    copies = [pltpu.make_async_copy(rms_ref, rms_hbm, sem.at[0])]
    for src, dst in ((params_ref, params_hbm), (momentum_ref, momentum_hbm)):
        step = src.shape[0] // SPLIT
        for i in range(SPLIT):
            part = pl.ds(i * step, step)
            copies.append(pltpu.make_async_copy(src.at[part], dst.at[part], sem.at[len(copies)]))
    for copy in copies:
        copy.start()
    for copy in copies:
        copy.wait()


def per_device(base, local, momentum):
    rows, columns = base.shape
    piece = columns // (SIDE * SIDE)
    number = piece // LANES
    half = rows // 2
    bf16 = functools.partial(pltpu.VMEM, dtype=jnp.bfloat16)
    vmem = pl.BlockSpec(memory_space=pltpu.VMEM)
    new_params, new_momentum, rms = pl.pallas_call(
        kernel,
        out_shape=(
            pltpu.VMEM((rows, columns), jnp.bfloat16),
            pltpu.VMEM((rows, piece), jnp.float32),
            pltpu.VMEM((1, 1), jnp.float32),
        ),
        in_specs=[pl.BlockSpec(memory_space=pltpu.HBM)] * 3,
        out_specs=(vmem, vmem, vmem),
        scratch_shapes=[
            bf16((rows, columns)),
            bf16((rows, columns)),
            pltpu.VMEM((rows, piece), jnp.float32),
            bf16((number, SIDE, SIDE, rows, LANES)),
            bf16((number, SIDE, rows, LANES)),
            bf16((number, SIDE, rows, LANES)),
            bf16((number, SIDE, half, LANES)),
            bf16((number, SIDE, half, LANES)),
            bf16((number, rows, LANES)),
            bf16((number, rows, LANES)),
            bf16((number, half, LANES)),
            bf16((number, half, LANES)),
            pltpu.VMEM((8, LANES), jnp.float32),
            pltpu.VMEM((4, 4, 8, LANES), jnp.float32),
            bf16((EARLY, 2, SIDE, rows, max(c[1] for c in CHUNKS[:EARLY]) * LANES)),
            pltpu.SemaphoreType.DMA((9 + EARLY,)),
            pltpu.SemaphoreType.DMA((len(CHUNKS) + 1,)),
            pltpu.SemaphoreType.DMA((RECEIVES,)),
        ],
        compiler_params=pltpu.CompilerParams(
            collective_id=0, has_side_effects=True, vmem_limit_bytes=24 * 2**20
        ),
        name="outer_step",
    )(*(pltpu.with_memory_space_constraint(a, pltpu.HBM) for a in (base, local, momentum)))
    hbm = pl.BlockSpec(memory_space=pltpu.HBM)
    new_params, new_momentum, rms = pl.pallas_call(
        write_out,
        out_shape=(
            pltpu.HBM((rows, columns), jnp.bfloat16),
            pltpu.HBM((rows, piece), jnp.float32),
            pltpu.HBM((1, 1), jnp.float32),
        ),
        in_specs=[vmem] * 3,
        out_specs=(hbm,) * 3,
        scratch_shapes=[pltpu.SemaphoreType.DMA((2 * SPLIT + 1,))],
        compiler_params=pltpu.CompilerParams(vmem_limit_bytes=2**20),
        name="write_out",
    )(*(pltpu.with_memory_space_constraint(a, pltpu.VMEM) for a in (new_params, new_momentum, rms)))
    return (new_params, new_momentum, rms[0, 0])


def solution(mesh):
    return jax.shard_map(
        per_device,
        mesh=mesh,
        in_specs=(P("fsdp", None), P("replica", "fsdp", None), P("fsdp", "replica")),
        out_specs=(P("fsdp", None), P("fsdp", "replica"), P()),
        check_vma=False,
    )
```
